512 devices in a mesh: tm: 4 (over y_lo, core), lat: 8 (over z), lon: 16 (over y_hi, x).
Axes of the slice: x: 4, y: 8 (y_hi: 4, y_lo: 2; y = y_hi * 2 + y_lo), z: 8, core: 2. Of those that a mesh axis runs over, the one named last changes fastest.
Arguments:
- fields: bfloat16 [64, 192, 192, 256], P(('tm', 'lon'), 'lat'), may hold values from -6 to 6
- scale_exponent: int32 [64], replicated, may hold values from -1 to 2
- level_mean: float32 [64], replicated, may hold values from -4 to 4
- level_spread: float32 [64], replicated, may hold values from 0.5 to 2
- row_offset: int32 [64], P('tm'), may hold values from 1 to 5
- column_offset: int32 [64], P('tm'), may hold values from 1 to 11
- patch_weight: bfloat16 [1024, 512], P(('tm', 'lat')), may hold values from -0.1875 to 0.1875
- attention_in: bfloat16 [512, 768], P(('tm', 'lat')), as said below
- attention_out: bfloat16 [256, 512], P(('tm', 'lat')), may hold values from -0.375 to 0.375
- hidden_in: bfloat16 [512, 1024], P(('tm', 'lat')), may hold values from -0.25 to 0.25
- hidden_out: bfloat16 [1024, 512], P(('tm', 'lat')), may hold values from -0.1875 to 0.1875
Outputs:
- encoded: bfloat16 [64, 48, 192, 512], P('tm', 'lat', 'lon')
The draws below stay inside these ranges and needn't reach their ends.
Inputs may be any that keep to these rules, and one draw needn't show every extreme that they name: `scale_exponent`: the exponent of the power of two that scales a variable. `attention_in`: query, key and value projections as column blocks in that order.
All inputs are finite; a program needn't handle non-finite values.
Results may differ from the reference program's by a relative error of at most 0.0059.
Values may be sent and summed in bfloat16 or wider, within the bound.
No kernel may reach another device: no remote copies, remote signals or barrier semaphores. Data moves between devices by JAX's collectives and lax.ppermute only.
A program may use at most 128 MiB of HBM per device.

```python
import math
import jax
import jax.numpy as jnp
from jax import lax

VARS = 64
P_SIZE = 4
D = 512
HEADS = 4
HEAD_DIM = 64
FF = 1024
WH = 6
WW = 12
TIMES = 64
NPH = 48
NPW = 192


def draw_attention_in(key, part):
    key = jax.random.fold_in(key, 7)
    first = jax.random.fold_in(key, 0)
    width = HEADS * HEAD_DIM
    full = jax.random.normal(first, (D, 3 * width), jnp.float32) * D ** (-0.5)
    return full.astype(jnp.bfloat16)


def touch_ends(result, own_key, least, high):
    spot = [jax.random.randint(jax.random.fold_in(own_key, axis), (), 0, length) for axis, length in enumerate(result.shape)]
    longest = result.shape.index(max(result.shape))
    next_to = spot[:longest] + [(spot[longest] + 1) % result.shape[longest]] + spot[longest + 1:]
    return result.at[tuple(spot)].set(least).at[tuple(next_to)].set(high)


def level_of(own_key, extent, pieces, smallest, top_value):
    def one(dim, shards_of):
        steps = jax.random.uniform(jax.random.fold_in(jax.random.fold_in(own_key, 6), dim), (shards_of,), jnp.float32, smallest / len(pieces), top_value / len(pieces))
        return jnp.repeat(jnp.exp(steps), extent[dim] // shards_of).reshape((-1,) + (1,) * (len(extent) - dim - 1))

    gain = one(*pieces[0])
    for cut in pieces[1:]:
        gain = gain * one(*cut)
    return gain


def gaussian(stream_key, extent, scale, bound, pieces=(), kind=jnp.bfloat16):
    array = scale * jax.random.normal(stream_key, extent, jnp.float32)
    if pieces:
        array = array * level_of(stream_key, extent, pieces, -0.22, 0.18)
    return jnp.clip(array, -bound, bound).astype(kind)


def setup_inputs(seed: int = 0) -> dict:
    streams_of = jax.random.split(jax.random.key(seed), 12)
    return {
        "fields": gaussian(streams_of[0], (TIMES, P_SIZE * NPH, NPW, P_SIZE * VARS), 1.0, 6.0, ((0, 64), (1, 8))),
        "scale_exponent": touch_ends(jax.random.randint(streams_of[1], (VARS,), -1, 3), jax.random.fold_in(streams_of[1], 1), -1, 2).astype(jnp.int32),
        "level_mean": gaussian(streams_of[2], (VARS,), 1.0, 4.0, (), jnp.float32),
        "level_spread": jnp.clip(jnp.exp(jax.random.uniform(streams_of[3], (VARS,), jnp.float32, math.log(0.5), math.log(2.0))), 0.5, 2.0),
        "row_offset": touch_ends(jax.random.randint(streams_of[4], (TIMES,), 1, WH), jax.random.fold_in(streams_of[4], 1), 1, WH - 1).astype(jnp.int32),
        "column_offset": touch_ends(jax.random.randint(streams_of[5], (TIMES,), 1, WW), jax.random.fold_in(streams_of[5], 1), 1, WW - 1).astype(jnp.int32),
        "patch_weight": gaussian(streams_of[6], (P_SIZE * P_SIZE * VARS, D), (P_SIZE * P_SIZE * VARS) ** -0.5, 0.1875, ((0, 32),)),
        "attention_in": draw_attention_in(jax.random.fold_in(streams_of[11], 71), 0),
        "attention_out": gaussian(streams_of[8], (HEADS * HEAD_DIM, D), (HEADS * HEAD_DIM) ** -0.5, 0.375, ((0, 32),)),
        "hidden_in": gaussian(streams_of[9], (D, FF), D ** -0.5, 0.25, ((0, 32),)),
        "hidden_out": gaussian(streams_of[10], (FF, D), FF ** -0.5, 0.1875, ((0, 32),)),
    }


epsilon = 1e-05

def layer_norm(values):
    values = values.astype(jnp.float32)
    center = values - lax.optimization_barrier(jnp.mean(values, axis=-1, keepdims=True))
    spread = lax.optimization_barrier(jnp.mean(center * center, axis=-1, keepdims=True))
    return (center * lax.rsqrt(spread + epsilon)).astype(jnp.bfloat16)

def attend(projected, allowed):
    width = HEADS * HEAD_DIM
    batch, count = (projected.shape[0], projected.shape[1])
    query_heads = projected[..., :width].astype(jnp.float32).reshape(batch, count, HEADS, HEAD_DIM)
    key_heads = projected[..., width:2 * width].astype(jnp.float32).reshape(batch, count, HEADS, HEAD_DIM)
    value_heads = projected[..., 2 * width:].astype(jnp.float32).reshape(batch, count, HEADS, HEAD_DIM)
    scores = jnp.einsum('bqhe,bkhe->bhqk', query_heads, key_heads) * HEAD_DIM ** (-0.5)
    scores = jnp.where(allowed[:, None], scores, -1e+30)
    attention_weights = jax.nn.softmax(scores, axis=-1).astype(jnp.bfloat16)
    mixed_values = jnp.einsum('bhqk,bkhe->bqhe', attention_weights.astype(jnp.float32), value_heads)
    return mixed_values.reshape(batch, count, width).astype(jnp.bfloat16)

def finish(tokens, mixed_values, attention_out, hidden_in, hidden_out):
    residual = tokens.astype(jnp.float32) + jnp.dot(mixed_values, attention_out, preferred_element_type=jnp.float32)
    inner = layer_norm(residual)
    expanded = jax.nn.gelu(jnp.dot(inner, hidden_in, preferred_element_type=jnp.float32), approximate=True)
    expanded = expanded.astype(jnp.bfloat16)
    return (residual + jnp.dot(expanded, hidden_out, preferred_element_type=jnp.float32)).astype(jnp.bfloat16)

def reference(fields, scale_exponent, level_mean, level_spread, row_offset, column_offset, patch_weight, attention_in, attention_out, hidden_in, hidden_out):
    chans = P_SIZE * VARS
    scale_factor = jnp.tile(jnp.exp2(scale_exponent.astype(jnp.float32)), P_SIZE)
    center = jnp.tile(level_mean, P_SIZE)
    spread = jnp.tile(level_spread, P_SIZE)
    table = patch_weight.astype(jnp.float32).reshape(P_SIZE, chans, D)
    window_rows = NPH // WH
    window_cols = NPW // WW

    def one_snapshot(item):
        raw, shift_row, shift_col = item
        normalized = ((raw.astype(jnp.float32) * scale_factor - center) / spread).astype(jnp.bfloat16)
        normalized = normalized.astype(jnp.float32).reshape(NPH, P_SIZE, NPW, chans)
        tokens = jnp.einsum('rpcv,pvd->rcd', normalized, table).astype(jnp.bfloat16)
        rolled = jnp.roll(tokens, (-shift_row, -shift_col), axis=(0, 1))
        grouped = rolled.reshape(window_rows, WH, window_cols, WW, D).transpose(0, 2, 1, 3, 4)
        grouped = grouped.reshape(window_rows * window_cols, WH * WW, D)
        row_place = jnp.arange(NPH, dtype=jnp.int32)
        north = (row_place >= NPH - shift_row).astype(jnp.int32)
        north = jnp.broadcast_to(north.reshape(window_rows, 1, WH, 1), (window_rows, window_cols, WH, WW))
        north = north.reshape(window_rows * window_cols, WH * WW)
        allowed = north[:, :, None] == north[:, None, :]
        normed = layer_norm(grouped)
        projected = jnp.dot(normed, attention_in, preferred_element_type=jnp.float32).astype(jnp.bfloat16)
        mixed_values = attend(projected, allowed)
        layer_result = finish(grouped, mixed_values, attention_out, hidden_in, hidden_out)
        layer_result = layer_result.reshape(window_rows, window_cols, WH, WW, D).transpose(0, 2, 1, 3, 4)
        layer_result = layer_result.reshape(NPH, NPW, D)
        return jnp.roll(layer_result, (shift_row, shift_col), axis=(0, 1))
    return lax.map(one_snapshot, (fields, row_offset, column_offset))
```

```python
import functools

import jax
import jax.numpy as jnp
from jax import lax
from jax.experimental import pallas as pl
from jax.experimental.pallas import tpu as pltpu
from jax.sharding import Mesh
from jax.sharding import PartitionSpec as P

P_SIZE = 4
HEAD_DIM = 64
HEADS = 4
WH = 6
WW = 12
PAD = 16
HALO = WH - 1
EPSILON = 1e-05
BF16 = jnp.bfloat16
F32 = jnp.float32
GROUP = 4


def dot(a, b):
    return jnp.dot(a, b, preferred_element_type=F32)


def dot_nt(a, b):
    return lax.dot_general(a, b, (((1,), (1,)), ((), ())), preferred_element_type=F32)


def one_hot(shape, column_of_row):
    row = lax.broadcasted_iota(jnp.int32, shape, 0)
    column = lax.broadcasted_iota(jnp.int32, shape, 1)
    return (column == column_of_row(row)).astype(F32).astype(BF16)


def layer_norm(values):
    center = values - jnp.mean(values, axis=-1, keepdims=True)
    spread = jnp.mean(center * center, axis=-1, keepdims=True)
    return (center * lax.rsqrt(spread + EPSILON)).astype(BF16)


def joined(ref, first, count):
    blocks = []
    for y in range(ref.shape[1]):
        for core in range(ref.shape[0]):
            block = ref[core, y, :, first : first + count, :]
            blocks.append(block.reshape(-1, block.shape[-1]))
    return jnp.concatenate(blocks, axis=0)


def embed_kernel(fields_ref, affine_ref, weight_ref, rows_ref, top_ref, bottom_ref, tiles_ref):
    rows = rows_ref.shape[0]
    columns = fields_ref.shape[1]
    chans = fields_ref.shape[2]
    raw = fields_ref[...].reshape(rows, P_SIZE, columns, chans)
    factor = affine_ref[0:1, :]
    shift = affine_ref[1:2, :]
    total = None
    for pixel in range(P_SIZE):
        part = raw[:, pixel].reshape(rows * columns, chans).astype(F32)
        part = (part * factor - shift).astype(BF16)
        table = weight_ref[pixel % 2, pixel // 2].reshape(chans, -1)
        product = dot(part, table)
        total = product if total is None else total + product
    tokens = total.astype(BF16)
    by_row = tokens.reshape(rows, columns, -1)
    rows_ref[...] = by_row
    top_ref[...] = by_row[:HALO]
    bottom_ref[...] = by_row[rows - HALO :]

    def source(k):
        tile, inner = k // (rows * WW), k % (rows * WW)
        return (inner // WW) * columns + tile * WW + inner % WW

    order = one_hot((rows * columns, rows * columns), source)
    tiles_ref[...] = dot(order, tokens).astype(BF16)


def embed(fields, affine, weight):
    pixel_rows, columns, chans = fields.shape
    rows = pixel_rows // P_SIZE
    width = weight.shape[-1]
    step = GROUP * WW
    return pl.pallas_call(
        embed_kernel,
        grid=(columns // step,),
        in_specs=[
            pl.BlockSpec((pixel_rows, step, chans), lambda g: (0, g, 0)),
            pl.BlockSpec(affine.shape, lambda g: (0, 0)),
            pl.BlockSpec(weight.shape, lambda g: (0,) * weight.ndim),
        ],
        out_specs=[
            pl.BlockSpec((rows, step, width), lambda g: (0, g, 0)),
            pl.BlockSpec((HALO, step, width), lambda g: (0, g, 0)),
            pl.BlockSpec((HALO, step, width), lambda g: (0, g, 0)),
            pl.BlockSpec((rows * step, width), lambda g: (g, 0)),
        ],
        out_shape=[
            jax.ShapeDtypeStruct((rows, columns, width), BF16),
            jax.ShapeDtypeStruct((HALO, columns, width), BF16),
            jax.ShapeDtypeStruct((HALO, columns, width), BF16),
            jax.ShapeDtypeStruct((rows * columns, width), BF16),
        ],
        compiler_params=pltpu.CompilerParams(vmem_limit_bytes=32 * 1024 * 1024),
        cost_estimate=pl.CostEstimate(
            flops=2 * rows * columns * P_SIZE * chans * width,
            bytes_accessed=fields.size * 2 + weight.size * 2 + 4 * rows * columns * width * 2,
            transcendentals=0,
        ),
        name="embed",
    )(fields, affine, weight)


def roll_matrix(columns, shift, scale):
    slots = columns // WW * PAD
    row = lax.broadcasted_iota(jnp.int32, (slots, columns), 0)
    column = lax.broadcasted_iota(jnp.int32, (slots, columns), 1)
    place = row % PAD
    want = (row // PAD) * WW + place + shift
    want = jnp.where(want >= columns, want - columns, want)
    hit = (want == column) & (place < WW)
    return jnp.where(hit, scale, 0.0).astype(BF16)


def project_kernel(spot_ref, rows_ref, weight_ref, query_ref, key_value_ref):
    rows, columns, features = rows_ref.shape
    width = query_ref.shape[-1]
    shift = spot_ref[1]
    matrix = joined(weight_ref, 0, weight_ref.shape[3])
    to_windows = roll_matrix(columns, shift, 1.0)
    to_queries = roll_matrix(columns, shift, HEAD_DIM**-0.5)
    for row in range(rows):
        normed = layer_norm(rows_ref[row].astype(F32))
        projected = dot(normed, matrix).astype(BF16)
        query_ref[row] = dot(to_queries, projected[:, :width]).astype(BF16)
        key_value_ref[row] = dot(to_windows, projected[:, width:]).astype(BF16)


def project(spot, rows_tokens, weight):
    rows, columns, features = rows_tokens.shape
    width = weight.shape[-1] // 3
    slots = columns // WW * PAD
    return pl.pallas_call(
        project_kernel,
        in_specs=[
            pl.BlockSpec(memory_space=pltpu.SMEM),
            pl.BlockSpec(memory_space=pltpu.VMEM),
            pl.BlockSpec(memory_space=pltpu.VMEM),
        ],
        out_shape=[
            jax.ShapeDtypeStruct((rows, slots, width), BF16),
            jax.ShapeDtypeStruct((rows, slots, 2 * width), BF16),
        ],
        compiler_params=pltpu.CompilerParams(vmem_limit_bytes=32 * 1024 * 1024),
        cost_estimate=pl.CostEstimate(
            flops=2 * rows * columns * (features + slots) * 3 * width,
            bytes_accessed=rows * columns * features * 2 + rows * slots * 3 * width * 2,
            transcendentals=0,
        ),
        name="project",
    )(spot, rows_tokens, weight)


def attend_kernel(
    spot_ref, north_ref, south_ref, query_ref, own_ref, weight_ref, mixed_ref, halo_ref, made_ref
):
    rows, slots, width = query_ref.shape
    columns = north_ref.shape[1]
    windows = slots // PAD
    split, shift, lat, last = spot_ref[0], spot_ref[1], spot_ref[2], spot_ref[3]

    matrix = joined(weight_ref, 0, weight_ref.shape[3])[:, width:]
    to_windows = roll_matrix(columns, shift, 1.0)
    for slot in range(rows):
        above = slot < rows - split
        north = north_ref[jnp.minimum(split - 1 + slot, HALO - 1)]
        south = south_ref[jnp.maximum(slot - (rows - split), 0)]
        values = jnp.where(above, north.astype(F32), south.astype(F32))
        projected = dot(layer_norm(values), matrix).astype(BF16)
        halo_ref[slot] = dot(to_windows, projected).astype(BF16)

    shape = (rows * PAD, 2 * rows * PAD)
    query = lax.broadcasted_iota(jnp.int32, shape, 0)
    key = lax.broadcasted_iota(jnp.int32, shape, 1)
    query_north = query // PAD < split
    is_halo = key >= rows * PAD
    key_row = jnp.where(is_halo, key - rows * PAD, key) // PAD
    key_north = key_row < jnp.where(is_halo, rows - split, split)
    beyond = jnp.where(is_halo, jnp.where(key_north, lat, last - lat), 1)
    same_band = query_north == key_north
    bias = jnp.where(same_band & (key % PAD < WW) & (beyond > 0), 0.0, -1e30)
    lane_head = lax.broadcasted_iota(jnp.int32, (rows * PAD, width), 1) // HEAD_DIM

    def window(m, carry):
        place = pl.ds(pl.multiple_of(m * PAD, PAD), PAD)
        queries = query_ref[:, place, :].reshape(rows * PAD, width)
        own = own_ref[:, place, :].reshape(rows * PAD, 2 * width)
        halo = halo_ref[:, place, :].reshape(rows * PAD, 2 * width)
        both = jnp.concatenate([own, halo], axis=0)
        zero = jnp.zeros_like(queries)
        stacked = jnp.concatenate(
            [jnp.where(lane_head == head, queries, zero) for head in range(HEADS)], axis=0
        )
        scores = dot_nt(stacked, both[:, :width]).reshape(HEADS, rows * PAD, -1) + bias[None]
        top = jnp.max(scores, axis=-1, keepdims=True)
        weights = jnp.exp(scores - top)
        total = jnp.sum(weights, axis=-1, keepdims=True)
        products = dot(weights.astype(BF16).reshape(HEADS * rows * PAD, -1), both[:, width:])
        products = products.reshape(HEADS, rows * PAD, width) / total
        mixed = products[0]
        for head in range(1, HEADS):
            mixed = jnp.where(lane_head == head, products[head], mixed)
        mixed = mixed.astype(BF16).reshape(rows, PAD, width)
        made_ref[:, pl.ds(pl.multiple_of((m + 1) * PAD, PAD), PAD), :] = mixed

        @pl.when(m == windows - 1)
        def _():
            made_ref[:, :PAD, :] = mixed

        return carry

    lax.fori_loop(0, windows, window, 0)

    def source(k):
        row, column = k // WW, k % WW
        inner = jnp.where(column < shift, column + WW - shift, PAD + column - shift)
        return row * (2 * PAD) + inner

    back = one_hot((rows * WW, rows * 2 * PAD), source)

    def tile(j, carry):
        pair = made_ref[:, pl.ds(pl.multiple_of(j * PAD, PAD), 2 * PAD), :]
        mixed_ref[j] = dot(back, pair.reshape(rows * 2 * PAD, width)).astype(BF16)
        return carry

    lax.fori_loop(0, windows, tile, 0)


def attend(spot, north, south, queries, own, weight):
    rows, slots, width = queries.shape
    windows = slots // PAD
    columns, features = north.shape[1:]
    vmem = pl.BlockSpec(memory_space=pltpu.VMEM)
    return pl.pallas_call(
        attend_kernel,
        in_specs=[pl.BlockSpec(memory_space=pltpu.SMEM)] + [vmem] * 5,
        out_shape=jax.ShapeDtypeStruct((windows, rows * WW, width), BF16),
        scratch_shapes=[
            pltpu.VMEM((rows, slots, 2 * width), BF16),
            pltpu.VMEM((rows, slots + PAD, width), BF16),
        ],
        compiler_params=pltpu.CompilerParams(vmem_limit_bytes=40 * 1024 * 1024),
        cost_estimate=pl.CostEstimate(
            flops=2 * rows * columns * (features + slots) * 2 * width
            + 4 * windows * HEADS * rows * PAD * 2 * rows * PAD * width,
            bytes_accessed=2 * north.size * 2 + rows * slots * 4 * width * 2,
            transcendentals=windows * HEADS * rows * PAD * 2 * rows * PAD,
        ),
        name="attend",
    )(spot, north, south, queries, own, weight)


def finish_kernel(tokens_ref, mixed_ref, out_weight_ref, shards_ref, encoded_ref, first_ref, second_ref):
    count, rows, columns, features = encoded_ref.shape
    half = features

    @pl.when(pl.program_id(0) == 0)
    def _():
        lines = 16
        first_ref[:, :half] = joined(shards_ref, 0, lines)
        first_ref[:, half:] = joined(shards_ref, lines, lines)
        second_ref[...] = joined(shards_ref, 2 * lines, 2 * lines)

    residual = tokens_ref[...].astype(F32) + dot(mixed_ref[...], out_weight_ref[...])
    inner = layer_norm(residual)
    expanded = jax.nn.gelu(dot(inner, first_ref[...]), approximate=True).astype(BF16)
    encoded = (residual + dot(expanded, second_ref[...])).astype(BF16)
    size = count * rows * columns

    def source(k):
        line, place = k // PAD, k % PAD
        return jnp.where(place < columns, line * columns + place, size)

    spread = one_hot((count * rows * PAD, size), source)
    padded = dot(spread, encoded).astype(BF16).reshape(count, rows, PAD, features)
    encoded_ref[...] = padded[:, :, :columns, :]


def finish(tokens, mixed, out_weight, shards):
    total, features = tokens.shape
    width = mixed.shape[1]
    times = total // (WH * WW)
    hidden = 2 * features
    block = GROUP * WH * WW
    return pl.pallas_call(
        finish_kernel,
        grid=(times // GROUP,),
        in_specs=[
            pl.BlockSpec((block, features), lambda g: (g, 0)),
            pl.BlockSpec((block, width), lambda g: (g, 0)),
            pl.BlockSpec(out_weight.shape, lambda g: (0, 0)),
            pl.BlockSpec(shards.shape, lambda g: (0,) * shards.ndim),
        ],
        out_specs=pl.BlockSpec((GROUP, WH, WW, features), lambda g: (g, 0, 0, 0)),
        out_shape=jax.ShapeDtypeStruct((times, WH, WW, features), BF16),
        scratch_shapes=[
            pltpu.VMEM((features, hidden), BF16),
            pltpu.VMEM((hidden, features), BF16),
        ],
        compiler_params=pltpu.CompilerParams(vmem_limit_bytes=40 * 1024 * 1024),
        cost_estimate=pl.CostEstimate(
            flops=2 * total * features * (width + 2 * hidden),
            bytes_accessed=total * (4 * features + 2 * width) + shards.size * 2,
            transcendentals=total * hidden,
        ),
        name="finish",
    )(tokens, mixed, out_weight, shards)


def copies(values, count):
    return jnp.broadcast_to(values[None], (count,) + values.shape)


def gather_far(shard):
    sizes = lax.axis_size("y_lo"), lax.axis_size("lat")
    found = lax.all_to_all(copies(shard, sizes[0] * sizes[1]), ("y_lo", "lat"), 0, 0, tiled=True)
    return found.reshape(sizes + shard.shape)


def gather_cores(shards):
    return lax.all_to_all(copies(shards, lax.axis_size("core")), "core", 0, 0, tiled=True)


def after(first, later):
    return lax.optimization_barrier((first, later))


def shards(
    fields,
    scale_exponent,
    level_mean,
    level_spread,
    row_offset,
    column_offset,
    patch_weight,
    attention_in,
    attention_out,
    hidden_in,
    hidden_out,
):
    features = patch_weight.shape[1]
    chans = fields.shape[3]
    lats = lax.axis_size("lat")
    lon = lax.axis_index(("y_hi", "x"))
    lat = lax.axis_index("lat")
    spot = jnp.stack(
        [
            lax.dynamic_index_in_dim(row_offset, lon, 0, False),
            lax.dynamic_index_in_dim(column_offset, lon, 0, False),
            lat,
            jnp.int32(lats - 1),
        ]
    )
    repeat = chans // level_mean.shape[0]
    affine = jnp.stack(
        [
            jnp.tile(jnp.exp2(scale_exponent.astype(F32)) / level_spread, repeat),
            jnp.tile(level_mean / level_spread, repeat),
        ]
    )

    patch_far = gather_far(patch_weight)
    patch_far, attention_in = after(patch_far, attention_in)
    patch_all = gather_cores(patch_far)
    project_far = gather_far(attention_in)
    patch_all, project_far = after(patch_all, project_far)
    project_all = gather_cores(project_far)

    rows_tokens, top, bottom, tiles = embed(fields[0], affine, patch_all)

    north = lax.ppermute(bottom, "lat", [(i, i + 1) for i in range(lats - 1)])
    south = lax.ppermute(top, "lat", [(i + 1, i) for i in range(lats - 1)])
    tiles = tiles.reshape((-1, WH * WW, features))
    tile_tokens = lax.all_to_all(tiles, ("y_hi", "x"), 0, 0, tiled=True)

    queries, own = project(spot, rows_tokens, project_all)

    half = hidden_in.shape[1] // 2
    packed = jnp.concatenate(
        [hidden_in[:, :half], hidden_in[:, half:], hidden_out, attention_out], axis=0
    )
    (north, south), packed = after((north, south), packed)
    hidden_far = gather_far(packed)
    mixed = attend(spot, north, south, queries, own, project_all)
    tile_mixed = lax.all_to_all(mixed, ("y_hi", "x"), 0, 0, tiled=True)

    hidden_all = gather_cores(hidden_far)
    out_rows = attention_out.shape[0]
    out_weight = hidden_all[:, :, :, -out_rows:, :].swapaxes(0, 1).reshape(-1, features)
    hidden_all = hidden_all[:, :, :, :-out_rows, :]
    return finish(
        tile_tokens.reshape(-1, features),
        tile_mixed.reshape(-1, tile_mixed.shape[-1]),
        out_weight,
        hidden_all,
    )


def solution(mesh):
    tm, lat, lon = (mesh.shape[name] for name in ("tm", "lat", "lon"))
    cores, across = 2, 4
    finer = Mesh(
        mesh.devices.reshape(tm // cores, cores, lat, lon // across, across),
        ("y_lo", "core", "lat", "y_hi", "x"),
    )
    time = ("y_lo", "core")
    in_specs = (
        P(time + ("y_hi", "x"), "lat", None, None),
        P(),
        P(),
        P(),
        P(time),
        P(time),
        P(time + ("lat",), None),
        P(time + ("lat",), None),
        P(time + ("lat",), None),
        P(time + ("lat",), None),
        P(time + ("lat",), None),
    )
    out_specs = P(time, "lat", ("y_hi", "x"), None)
    return jax.shard_map(shards, mesh=finer, in_specs=in_specs, out_specs=out_specs, check_vma=False)
```

```python
import functools

import jax
import jax.numpy as jnp
from jax import lax
from jax.experimental import pallas as pl
from jax.experimental.pallas import tpu as pltpu
from jax.sharding import Mesh
from jax.sharding import PartitionSpec as P

P_SIZE = 4
HEAD_DIM = 64
HEADS = 4
WH = 6
WW = 12
PAD = 16
HALO = WH - 1
BAND = 8
EPSILON = 1e-05
BF16 = jnp.bfloat16
F32 = jnp.float32
GROUP = 4
ATTEND_COST = 1
EMBED_COST = 2 * 10**10
CHOOSE_COST = 3 * 10**10
LINES = 16


def dot(a, b):
    return jnp.dot(a, b, preferred_element_type=F32)


def dot_nt(a, b):
    return lax.dot_general(a, b, (((1,), (1,)), ((), ())), preferred_element_type=F32)


def one_hot(shape, column_of_row):
    row = lax.broadcasted_iota(jnp.int32, shape, 0)
    column = lax.broadcasted_iota(jnp.int32, shape, 1)
    return (column == column_of_row(row)).astype(F32).astype(BF16)


def layer_norm(values):
    center = values - jnp.mean(values, axis=-1, keepdims=True)
    spread = jnp.mean(center * center, axis=-1, keepdims=True)
    return (center * lax.rsqrt(spread + EPSILON)).astype(BF16)


def position():
    lon = lax.axis_index("y_hi") * lax.axis_size("x") + lax.axis_index("x")
    return {
        "core": lax.axis_index("core"),
        "y_lo": lax.axis_index("y_lo"),
        "lat": lax.axis_index("lat"),
        "last": lax.axis_size("lat") - 1,
        "lon": lon,
    }


def place(core_swapped, y_swapped):
    here = position()
    core, y = here["core"], here["y_lo"]
    core = 1 - core if core_swapped else core
    y = 1 - y if y_swapped else y
    return y * 2 + core


def collect(shards, target_ref, columns=slice(None)):
    for spot, block in shards:
        block = block.reshape(-1, block.shape[-1])
        start = pl.multiple_of(spot * block.shape[0], block.shape[0])
        target_ref[pl.ds(start, block.shape[0]), columns] = block


def parts(refs, first, count, half):
    return [
        (place(swapped, y), ref[:, y * half + first : y * half + first + count])
        for swapped, ref in enumerate(refs)
        for y in range(2)
    ]


def pack_kernel(hidden_in_ref, hidden_out_ref, attention_out_ref, attention_in_ref, packed_ref):
    lines, features = LINES, packed_ref.shape[1]
    short = lines // 2
    width = attention_in_ref.shape[1] // 3
    packed_ref[:lines] = hidden_in_ref[:, :features]
    packed_ref[lines : 2 * lines] = hidden_in_ref[:, features:]
    packed_ref[2 * lines : 4 * lines] = hidden_out_ref[...]
    packed_ref[4 * lines : 5 * lines] = attention_in_ref[:, width:]
    query = attention_in_ref[:, :width].astype(F32)
    query = jnp.concatenate([query[:short], query[short:]], axis=1)
    out = attention_out_ref[...].astype(F32)
    packed_ref[5 * lines :] = jnp.concatenate([out, query], axis=0).astype(BF16)


def pack(hidden_in, hidden_out, attention_out, attention_in):
    return pl.pallas_call(
        pack_kernel,
        in_specs=[pl.BlockSpec(memory_space=pltpu.VMEM)] * 4,
        out_shape=jax.ShapeDtypeStruct((6 * LINES, hidden_out.shape[1]), BF16),
        name="pack",
    )(hidden_in, hidden_out, attention_out, attention_in)


def join_kernel(own_ref, swapped_ref, joined_ref):
    far = 4 * LINES
    near = own_ref.shape[0] - far
    joined_ref[:far] = own_ref[:far]
    joined_ref[far : 2 * far] = swapped_ref[:far]
    joined_ref[2 * far : 2 * far + near] = own_ref[far:]
    joined_ref[2 * far + near :] = swapped_ref[far:]


def join(own, swapped):
    return pl.pallas_call(
        join_kernel,
        in_specs=[pl.BlockSpec(memory_space=pltpu.VMEM)] * 2,
        out_shape=jax.ShapeDtypeStruct((2 * own.shape[0], own.shape[1]), BF16),
        name="join",
    )(own, swapped)


def normalize_kernel(fields_ref, affine_ref, normalized_ref):
    factor = affine_ref[0:1, :]
    shift = affine_ref[1:2, :]
    normalized_ref[...] = (fields_ref[...].astype(F32) * factor - shift).astype(BF16)


def normalize(fields, affine):
    pixel_rows, columns, chans = fields.shape
    return pl.pallas_call(
        normalize_kernel,
        grid=(pixel_rows // P_SIZE,),
        in_specs=[
            pl.BlockSpec((P_SIZE, columns, chans), lambda g: (g, 0, 0)),
            pl.BlockSpec(affine.shape, lambda g: (0, 0)),
        ],
        out_specs=pl.BlockSpec((P_SIZE, columns, chans), lambda g: (g, 0, 0)),
        out_shape=jax.ShapeDtypeStruct(fields.shape, BF16),
        compiler_params=pltpu.CompilerParams(vmem_limit_bytes=12 * 1024 * 1024),
        name="normalize",
    )(fields, affine)


def embed_kernel(
    fields_ref,
    weight_ref,
    other_ref,
    rows_ref,
    top_ref,
    bottom_ref,
    tiles_ref,
    table_ref,
):
    rows = rows_ref.shape[0]

    @pl.when(pl.program_id(0) == 0)
    def _():
        for swapped, ref in enumerate((weight_ref, other_ref)):
            for y in range(ref.shape[0]):
                core = place(swapped, 0) % 2
                table_ref[2 * y + core] = ref[y].reshape(table_ref.shape[1:])

    columns = fields_ref.shape[1]
    chans = fields_ref.shape[2]
    normalized = fields_ref[...].reshape(rows, P_SIZE, columns, chans)
    total = None
    for pixel in range(P_SIZE):
        product = dot(normalized[:, pixel].reshape(rows * columns, chans), table_ref[pixel])
        total = product if total is None else total + product
    tokens = total.astype(BF16)
    by_row = tokens.reshape(rows, columns, -1)
    rows_ref[...] = by_row
    top_ref[...] = by_row[:HALO]
    bottom_ref[...] = by_row[rows - HALO :]

    def source(k):
        tile, inner = k // (rows * WW), k % (rows * WW)
        return (inner // WW) * columns + tile * WW + inner % WW

    order = one_hot((rows * columns, rows * columns), source)
    tiles_ref[...] = dot(order, tokens).astype(BF16)


def embed(fields, weight, other):
    pixel_rows, columns, chans = fields.shape
    rows = pixel_rows // P_SIZE
    width = weight.shape[-1]
    step = GROUP * WW
    return pl.pallas_call(
        embed_kernel,
        grid=(columns // step,),
        in_specs=[
            pl.BlockSpec((pixel_rows, step, chans), lambda g: (0, g, 0)),
            pl.BlockSpec(weight.shape, lambda g: (0,) * weight.ndim),
            pl.BlockSpec(weight.shape, lambda g: (0,) * weight.ndim),
        ],
        out_specs=[
            pl.BlockSpec((rows, step, width), lambda g: (0, g, 0)),
            pl.BlockSpec((HALO, step, width), lambda g: (0, g, 0)),
            pl.BlockSpec((HALO, step, width), lambda g: (0, g, 0)),
            pl.BlockSpec((rows * step, width), lambda g: (g, 0)),
        ],
        out_shape=[
            jax.ShapeDtypeStruct((rows, columns, width), BF16),
            jax.ShapeDtypeStruct((HALO, columns, width), BF16),
            jax.ShapeDtypeStruct((HALO, columns, width), BF16),
            jax.ShapeDtypeStruct((rows * columns, width), BF16),
        ],
        scratch_shapes=[pltpu.VMEM((P_SIZE, chans, width), BF16)],
        compiler_params=pltpu.CompilerParams(vmem_limit_bytes=16 * 1024 * 1024),
        cost_estimate=pl.CostEstimate(
            flops=EMBED_COST,
            bytes_accessed=0,
            transcendentals=0,
        ),
        name="embed",
    )(fields, weight, other)


def roll_matrix(columns, shift, scale):
    slots = columns // WW * PAD
    row = lax.broadcasted_iota(jnp.int32, (slots, columns), 0)
    column = lax.broadcasted_iota(jnp.int32, (slots, columns), 1)
    place = row % PAD
    want = (row // PAD) * WW + place + shift
    want = jnp.where(want >= columns, want - columns, want)
    hit = (want == column) & (place < WW)
    return jnp.where(hit, scale, 0.0).astype(BF16)


def project_kernel(
    column_offset_ref,
    rows_ref,
    weight_ref,
    other_ref,
    query_ref,
    key_value_ref,
    matrix_ref,
    query_matrix_ref,
):
    rows, columns, features = rows_ref.shape
    width = query_ref.shape[-1]
    shift = column_offset_ref[position()["lon"]]
    refs = weight_ref, other_ref
    collect(parts(refs, 0, LINES, 2 * LINES), matrix_ref)
    for spot, block in parts(refs, LINES, LINES, 2 * LINES):
        block = block.astype(F32)[:, LINES // 2 :]
        block = jnp.concatenate([block[..., :width], block[..., width:]], axis=1)
        collect([(spot, block.reshape(-1, width).astype(BF16))], query_matrix_ref)
    matrix = jnp.concatenate([query_matrix_ref[...], matrix_ref[...]], axis=1)
    to_windows = roll_matrix(columns, shift, 1.0)
    to_queries = roll_matrix(columns, shift, HEAD_DIM**-0.5)
    for row in range(rows):
        normed = layer_norm(rows_ref[row].astype(F32))
        projected = dot(normed, matrix).astype(BF16)
        query_ref[row] = dot(to_queries, projected[:, :width]).astype(BF16)
        key_value_ref[row] = dot(to_windows, projected[:, width:]).astype(BF16)


def project(column_offset, rows_tokens, weights):
    rows, columns, features = rows_tokens.shape
    width = HEADS * HEAD_DIM
    slots = columns // WW * PAD
    return pl.pallas_call(
        project_kernel,
        in_specs=[pl.BlockSpec(memory_space=pltpu.SMEM)]
        + [pl.BlockSpec(memory_space=pltpu.VMEM)] * 3,
        out_shape=[
            jax.ShapeDtypeStruct((rows, slots, width), BF16),
            jax.ShapeDtypeStruct((rows, slots, 2 * width), BF16),
            jax.ShapeDtypeStruct((features, 2 * width), BF16),
        ],
        scratch_shapes=[pltpu.VMEM((features, width), BF16)],
        compiler_params=pltpu.CompilerParams(vmem_limit_bytes=20 * 1024 * 1024),
        cost_estimate=pl.CostEstimate(
            flops=2 * rows * columns * (features + slots) * 3 * width,
            bytes_accessed=rows * columns * features * 2 + rows * slots * 3 * width * 2,
            transcendentals=0,
        ),
        name="project",
    )(column_offset, rows_tokens, *weights)


def choose_kernel(row_offset_ref, north_ref, south_ref, normed_ref):
    rows = normed_ref.shape[0]
    split = row_offset_ref[position()["lon"]]
    for slot in range(rows):
        north = north_ref[jnp.minimum(split - 1 + slot, HALO - 1)]
        south = south_ref[jnp.maximum(slot - (rows - split), 0)]
        values = jnp.where(slot < rows - split, north.astype(F32), south.astype(F32))
        normed_ref[slot] = layer_norm(values)


def choose(row_offset, north, south):
    columns, features = north.shape[1:]
    vmem = pl.BlockSpec(memory_space=pltpu.VMEM)
    return pl.pallas_call(
        choose_kernel,
        in_specs=[pl.BlockSpec(memory_space=pltpu.SMEM), vmem, vmem],
        out_shape=jax.ShapeDtypeStruct((WH, columns, features), BF16),
        compiler_params=pltpu.CompilerParams(vmem_limit_bytes=8 * 1024 * 1024),
        cost_estimate=pl.CostEstimate(flops=CHOOSE_COST, bytes_accessed=0, transcendentals=0),
        name="choose",
    )(row_offset, north, south)


def attend_kernel(
    row_offset_ref,
    column_offset_ref,
    normed_ref,
    query_ref,
    own_ref,
    matrix_ref,
    mixed_ref,
    keys_ref,
    made_ref,
):
    rows, slots, width = query_ref.shape
    columns = normed_ref.shape[1]
    windows = slots // PAD
    here = position()
    lat, last = here["lat"], here["last"]
    split, shift = row_offset_ref[here["lon"]], column_offset_ref[here["lon"]]
    half = keys_ref.shape[0] // 2
    for band in range(2):
        for slot in range(rows, half):
            keys_ref[band * half + slot] = jnp.zeros(keys_ref.shape[1:], BF16)
    for row in range(rows):
        spot = jnp.where(row < split, row + rows - split, half + row - split)
        keys_ref[spot] = own_ref[row]

    matrix = matrix_ref[...]
    to_windows = roll_matrix(columns, shift, 1.0)
    for slot in range(rows):
        projected = dot(normed_ref[slot], matrix).astype(BF16)
        spot = jnp.where(slot < rows - split, slot, half + slot)
        keys_ref[spot] = dot(to_windows, projected).astype(BF16)

    shape = (rows, PAD, half * PAD)
    north_query = lax.broadcasted_iota(jnp.int32, shape, 0) < split
    key = lax.broadcasted_iota(jnp.int32, shape, 2)
    key_row = key // PAD
    from_north = key_row < rows - split
    beyond = jnp.where(
        north_query, jnp.where(from_north, lat, 1), jnp.where(from_north, 1, last - lat)
    )
    bias = jnp.where((key_row < rows) & (key % PAD < WW) & (beyond > 0), 0.0, -1e30)
    lane_head = lax.broadcasted_iota(jnp.int32, (rows * PAD, width), 1) // HEAD_DIM

    def window(m):
        here = pl.ds(pl.multiple_of(m * PAD, PAD), PAD)
        queries = query_ref[:, here, :].reshape(rows * PAD, width)
        keys = keys_ref[:, here, :].reshape(2 * half * PAD, 2 * width)
        zero = jnp.zeros_like(queries)
        stacked = jnp.concatenate(
            [jnp.where(lane_head == head, queries, zero) for head in range(HEADS)], axis=0
        )
        scores = dot_nt(stacked, keys[:, :width]).reshape(HEADS, rows, PAD, 2 * half * PAD)
        scores = jnp.where(north_query[None], scores[..., : half * PAD], scores[..., half * PAD :])
        scores = scores + bias[None]
        weights = jnp.exp(scores - jnp.max(scores, axis=-1, keepdims=True))
        weights = weights * (1.0 / jnp.sum(weights, axis=-1, keepdims=True))
        weights = jnp.concatenate(
            [jnp.where(north_query[None], weights, 0.0), jnp.where(north_query[None], 0.0, weights)],
            axis=-1,
        ).astype(BF16)
        products = dot(weights.reshape(HEADS * rows * PAD, -1), keys[:, width:])
        products = products.reshape(HEADS, rows * PAD, width)
        mixed = products[0]
        for head in range(1, HEADS):
            mixed = jnp.where(lane_head == head, products[head], mixed)
        mixed = mixed.astype(BF16).reshape(rows, PAD, width)
        made_ref[:, pl.ds(pl.multiple_of((m + 1) * PAD, PAD), PAD), :] = mixed

    def some_windows(step, carry):
        for inner in range(GROUP):
            window(step * GROUP + inner)
        return carry

    lax.fori_loop(0, windows // GROUP, some_windows, 0)
    made_ref[:, :PAD, :] = made_ref[:, windows * PAD :, :]

    def source(k):
        row, column = k // WW, k % WW
        inner = jnp.where(column < shift, column + WW - shift, PAD + column - shift)
        return row * (2 * PAD) + inner

    back = one_hot((rows * WW, rows * 2 * PAD), source)
    for j in range(windows):
        pair = made_ref[:, j * PAD : (j + 2) * PAD, :]
        mixed_ref[j] = dot(back, pair.reshape(rows * 2 * PAD, width)).astype(BF16)


def attend(row_offset, column_offset, normed, queries, own, matrix):
    rows, slots, width = queries.shape
    windows = slots // PAD
    columns, features = normed.shape[1:]
    vmem = pl.BlockSpec(memory_space=pltpu.VMEM)
    return pl.pallas_call(
        attend_kernel,
        in_specs=[pl.BlockSpec(memory_space=pltpu.SMEM)] * 2 + [vmem] * 4,
        out_shape=jax.ShapeDtypeStruct((windows, rows * WW, width), BF16),
        scratch_shapes=[
            pltpu.VMEM((2 * BAND, slots, 2 * width), BF16),
            pltpu.VMEM((rows, slots + PAD, width), BF16),
        ],
        compiler_params=pltpu.CompilerParams(vmem_limit_bytes=24 * 1024 * 1024),
        cost_estimate=pl.CostEstimate(
            flops=ATTEND_COST * 2 * rows * columns * (features + slots) * 2 * width
            + ATTEND_COST * 4 * windows * HEADS * rows * PAD * 2 * rows * PAD * width,
            bytes_accessed=normed.size * 2 + rows * slots * 4 * width * 2,
            transcendentals=windows * HEADS * rows * PAD * 2 * rows * PAD,
        ),
        name="attend",
    )(row_offset, column_offset, normed, queries, own, matrix)


def finish_kernel(
    tokens_ref,
    mixed_ref,
    hidden_ref,
    hidden_other_ref,
    near_ref,
    near_other_ref,
    encoded_ref,
    out_ref,
    first_ref,
    second_ref,
):
    count, cells, features = tokens_ref.shape
    lines = LINES

    @pl.when(pl.program_id(0) == 0)
    def _():
        refs = hidden_ref, hidden_other_ref
        collect(parts(refs, 0, lines, 4 * lines), first_ref, slice(0, features))
        collect(parts(refs, lines, lines, 4 * lines), first_ref, slice(features, 2 * features))
        collect(parts(refs, 2 * lines, 2 * lines, 4 * lines), second_ref)
        for spot, block in parts((near_ref, near_other_ref), lines, lines, 2 * lines):
            block = block.astype(F32)[:, : lines // 2].reshape(-1, features)
            collect([(spot, block.astype(BF16))], out_ref)

    tokens = tokens_ref[...].reshape(count * cells, features).astype(F32)
    mixed = mixed_ref[...].reshape(count * cells, -1)
    residual = tokens + dot(mixed, out_ref[...])
    inner = layer_norm(residual)
    expanded = jax.nn.gelu(dot(inner, first_ref[...]), approximate=True).astype(BF16)
    encoded = (residual + dot(expanded, second_ref[...])).astype(BF16)
    encoded_ref[...] = encoded.reshape(count, cells, features)


def finish(tokens, mixed, weights):
    tiles, cells, features = tokens.shape
    width = mixed.shape[2]
    hidden = 2 * features
    return pl.pallas_call(
        finish_kernel,
        grid=(tiles // GROUP,),
        in_specs=[
            pl.BlockSpec((GROUP, cells, features), lambda g: (g, 0, 0)),
            pl.BlockSpec((GROUP, cells, width), lambda g: (g, 0, 0)),
        ]
        + [pl.BlockSpec(weight.shape, lambda g: (0, 0, 0)) for weight in weights],
        out_specs=pl.BlockSpec((GROUP, cells, features), lambda g: (g, 0, 0)),
        out_shape=jax.ShapeDtypeStruct((tiles, cells, features), BF16),
        scratch_shapes=[
            pltpu.VMEM((width, features), BF16),
            pltpu.VMEM((features, hidden), BF16),
            pltpu.VMEM((hidden, features), BF16),
        ],
        compiler_params=pltpu.CompilerParams(vmem_limit_bytes=24 * 1024 * 1024),
        cost_estimate=pl.CostEstimate(
            flops=2 * tiles * cells * features * (width + 2 * hidden),
            bytes_accessed=tiles * cells * (4 * features + 2 * width) + weights[0].size * 6,
            transcendentals=tiles * cells * hidden,
        ),
        name="finish",
    )(tokens, mixed, *weights)


def turn_kernel(encoded_ref, turned_ref):
    count, cells, features = encoded_ref.shape
    size = count * cells
    order = one_hot((size, size), lambda k: (k % count) * cells + k // count)
    flat = encoded_ref[...].astype(F32).reshape(size, features).astype(BF16)
    turned_ref[...] = dot(order, flat).astype(BF16).reshape(cells, count, features)


def turn(encoded):
    count, cells, features = encoded.shape
    block = 24
    return pl.pallas_call(
        turn_kernel,
        grid=(cells // block,),
        in_specs=[pl.BlockSpec((count, block, features), lambda g: (0, g, 0))],
        out_specs=pl.BlockSpec((block, count, features), lambda g: (g, 0, 0)),
        out_shape=jax.ShapeDtypeStruct((cells, count, features), BF16),
        compiler_params=pltpu.CompilerParams(vmem_limit_bytes=12 * 1024 * 1024),
        name="turn",
    )(encoded)


def copies(values, count):
    return jnp.broadcast_to(values[None], (count,) + values.shape)


def gather_far(shard):
    sizes = lax.axis_size("y_lo"), lax.axis_size("lat")
    found = lax.all_to_all(copies(shard, sizes[0] * sizes[1]), ("y_lo", "lat"), 0, 0, tiled=True)
    return found.reshape(sizes + shard.shape)


def swap(values, axis):
    return lax.ppermute(values, axis, [(0, 1), (1, 0)])


def after(first, *later):
    return lax.optimization_barrier((first,) + later)


def shards(
    fields,
    scale_exponent,
    level_mean,
    level_spread,
    row_offset,
    column_offset,
    patch_weight,
    attention_in,
    attention_out,
    hidden_in,
    hidden_out,
):
    features = patch_weight.shape[1]
    chans = fields.shape[3]
    lats = lax.axis_size("lat")
    repeat = chans // level_mean.shape[0]
    affine = jnp.stack(
        [
            jnp.tile(jnp.exp2(scale_exponent.astype(F32)) / level_spread, repeat),
            jnp.tile(level_mean / level_spread, repeat),
        ]
    )

    normalized = normalize(fields[0], affine)
    packed = pack(hidden_in, hidden_out, attention_out, attention_in)
    packed = join(packed, swap(packed, "y_lo"))
    rest = lax.all_gather(packed, "lat", axis=0)
    patch = gather_far(patch_weight)
    patch, normalized = after(patch, normalized)

    rows_tokens, top, bottom, tiles = embed(normalized, patch, swap(patch, "core"))
    _, rest = after(rows_tokens, rest)
    north = lax.ppermute(bottom, "lat", [(i, i + 1) for i in range(lats - 1)])
    south = lax.ppermute(top, "lat", [(i + 1, i) for i in range(lats - 1)])
    near = rest[:, 8 * LINES :]
    near = near, swap(near, "core")
    window_queries, own, matrix = project(column_offset, rows_tokens, near)
    normed = choose(row_offset, north, south)
    _, hidden_weight = after(matrix, rest[:, : 8 * LINES])
    mixed = attend(row_offset, column_offset, normed, window_queries, own, matrix)
    encoded = finish(tiles.reshape(-1, WH * WW, features), mixed, (hidden_weight, swap(hidden_weight, "core")) + near)
    encoded = turn(lax.all_to_all(encoded, ("y_hi", "x"), 0, 0, tiled=True))
    return encoded.reshape(WH, WW, -1, features).transpose(2, 0, 1, 3)


def solution(mesh):
    tm, lat, lon = (mesh.shape[name] for name in ("tm", "lat", "lon"))
    cores, across = 2, 4
    finer = Mesh(
        mesh.devices.reshape(tm // cores, cores, lat, lon // across, across),
        ("y_lo", "core", "lat", "y_hi", "x"),
    )
    time = ("y_lo", "core")
    in_specs = (
        P(time + ("y_hi", "x"), "lat", None, None),
        P(),
        P(),
        P(),
        P(time),
        P(time),
        P(time + ("lat",), None),
        P(time + ("lat",), None),
        P(time + ("lat",), None),
        P(time + ("lat",), None),
        P(time + ("lat",), None),
    )
    out_specs = P(time, "lat", ("y_hi", "x"), None)
    return jax.shard_map(shards, mesh=finer, in_specs=in_specs, out_specs=out_specs, check_vma=False)
```

```python
import functools

import jax
import jax.numpy as jnp
from jax import lax
from jax.experimental import pallas as pl
from jax.experimental.pallas import tpu as pltpu
from jax.sharding import Mesh
from jax.sharding import PartitionSpec as P

P_SIZE = 4
HEAD_DIM = 64
HEADS = 4
WH = 6
WW = 12
PAD = 16
HALO = WH - 1
BAND = 8
EPSILON = 1e-05
BF16 = jnp.bfloat16
F32 = jnp.float32
GROUP = 4
ATTEND_COST = 1
EMBED_COST = 6 * 10**9
CHOOSE_COST = 8 * 10**9
LINES = 16


def dot(a, b):
    return jnp.dot(a, b, preferred_element_type=F32)


def dot_nt(a, b):
    return lax.dot_general(a, b, (((1,), (1,)), ((), ())), preferred_element_type=F32)


def one_hot(shape, column_of_row):
    row = lax.broadcasted_iota(jnp.int32, shape, 0)
    column = lax.broadcasted_iota(jnp.int32, shape, 1)
    return (column == column_of_row(row)).astype(F32).astype(BF16)


def layer_norm(values):
    center = values - jnp.mean(values, axis=-1, keepdims=True)
    spread = jnp.mean(center * center, axis=-1, keepdims=True)
    return (center * lax.rsqrt(spread + EPSILON)).astype(BF16)


def position():
    lon = lax.axis_index("y_hi") * lax.axis_size("x") + lax.axis_index("x")
    return {
        "core": lax.axis_index("core"),
        "y_lo": lax.axis_index("y_lo"),
        "lat": lax.axis_index("lat"),
        "last": lax.axis_size("lat") - 1,
        "lon": lon,
    }


def place(core_swapped, y_swapped):
    here = position()
    core, y = here["core"], here["y_lo"]
    core = 1 - core if core_swapped else core
    y = 1 - y if y_swapped else y
    return y * 2 + core


def collect(shards, target_ref, columns=slice(None)):
    for spot, block in shards:
        block = block.reshape(-1, block.shape[-1])
        start = pl.multiple_of(spot * block.shape[0], block.shape[0])
        target_ref[pl.ds(start, block.shape[0]), columns] = block


def parts(refs, first, count, half):
    return [
        (place(swapped, y), ref[:, y * half + first : y * half + first + count])
        for swapped, ref in enumerate(refs)
        for y in range(2)
    ]


def pack_kernel(hidden_in_ref, hidden_out_ref, attention_out_ref, attention_in_ref, packed_ref):
    lines, features = LINES, packed_ref.shape[1]
    short = lines // 2
    width = attention_in_ref.shape[1] // 3
    packed_ref[:lines] = hidden_in_ref[:, :features]
    packed_ref[lines : 2 * lines] = hidden_in_ref[:, features:]
    packed_ref[2 * lines : 4 * lines] = hidden_out_ref[...]
    packed_ref[4 * lines : 5 * lines] = attention_in_ref[:, width:]
    query = attention_in_ref[:, :width].astype(F32)
    query = jnp.concatenate([query[:short], query[short:]], axis=1)
    out = attention_out_ref[...].astype(F32)
    packed_ref[5 * lines :] = jnp.concatenate([out, query], axis=0).astype(BF16)


def pack(hidden_in, hidden_out, attention_out, attention_in):
    return pl.pallas_call(
        pack_kernel,
        in_specs=[pl.BlockSpec(memory_space=pltpu.VMEM)] * 4,
        out_shape=jax.ShapeDtypeStruct((6 * LINES, hidden_out.shape[1]), BF16),
        name="pack",
    )(hidden_in, hidden_out, attention_out, attention_in)


def join_kernel(own_ref, swapped_ref, early_ref, late_ref):
    size = 2 * LINES
    for y, ref in enumerate((own_ref, swapped_ref)):
        early_ref[y * size : (y + 1) * size] = ref[2 * size :]
        early_ref[(2 + y) * size : (3 + y) * size] = ref[:size]
        late_ref[y * size : (y + 1) * size] = ref[size : 2 * size]
    late_ref[2 * size :] = jnp.zeros((2 * size, own_ref.shape[1]), BF16)


def join(own, swapped):
    shape = jax.ShapeDtypeStruct((8 * LINES, own.shape[1]), BF16)
    return pl.pallas_call(
        join_kernel,
        in_specs=[pl.BlockSpec(memory_space=pltpu.VMEM)] * 2,
        out_shape=[shape, shape],
        name="join",
    )(own, swapped)


def embed_kernel(
    fields_ref,
    affine_ref,
    weight_ref,
    other_ref,
    rows_ref,
    top_ref,
    bottom_ref,
    tiles_ref,
    table_ref,
):
    rows = rows_ref.shape[0]

    @pl.when(pl.program_id(0) == 0)
    def _():
        for swapped, ref in enumerate((weight_ref, other_ref)):
            for y in range(ref.shape[0]):
                core = place(swapped, 0) % 2
                table_ref[2 * y + core] = ref[y].reshape(table_ref.shape[1:])

    columns = fields_ref.shape[1]
    chans = fields_ref.shape[2]
    raw = fields_ref[...].reshape(rows, P_SIZE, columns, chans)
    factor = affine_ref[0:1, :]
    shift = affine_ref[1:2, :]
    total = None
    for pixel in range(P_SIZE):
        part = raw[:, pixel].reshape(rows * columns, chans).astype(F32)
        part = (part * factor - shift).astype(BF16)
        product = dot(part, table_ref[pixel])
        total = product if total is None else total + product
    tokens = total.astype(BF16)
    by_row = tokens.reshape(rows, columns, -1)
    rows_ref[...] = by_row
    top_ref[...] = by_row[:HALO]
    bottom_ref[...] = by_row[rows - HALO :]

    def source(k):
        tile, inner = k // (rows * WW), k % (rows * WW)
        return (inner // WW) * columns + tile * WW + inner % WW

    order = one_hot((rows * columns, rows * columns), source)
    tiles_ref[...] = dot(order, tokens).astype(BF16)


def embed(fields, affine, weight, other):
    pixel_rows, columns, chans = fields.shape
    rows = pixel_rows // P_SIZE
    width = weight.shape[-1]
    step = GROUP * WW
    return pl.pallas_call(
        embed_kernel,
        grid=(columns // step,),
        in_specs=[
            pl.BlockSpec((pixel_rows, step, chans), lambda g: (0, g, 0)),
            pl.BlockSpec(affine.shape, lambda g: (0, 0)),
            pl.BlockSpec(weight.shape, lambda g: (0,) * weight.ndim),
            pl.BlockSpec(weight.shape, lambda g: (0,) * weight.ndim),
        ],
        out_specs=[
            pl.BlockSpec((rows, step, width), lambda g: (0, g, 0)),
            pl.BlockSpec((HALO, step, width), lambda g: (0, g, 0)),
            pl.BlockSpec((HALO, step, width), lambda g: (0, g, 0)),
            pl.BlockSpec((rows * step, width), lambda g: (g, 0)),
        ],
        out_shape=[
            jax.ShapeDtypeStruct((rows, columns, width), BF16),
            jax.ShapeDtypeStruct((HALO, columns, width), BF16),
            jax.ShapeDtypeStruct((HALO, columns, width), BF16),
            jax.ShapeDtypeStruct((rows * columns, width), BF16),
        ],
        scratch_shapes=[pltpu.VMEM((P_SIZE, chans, width), BF16)],
        compiler_params=pltpu.CompilerParams(vmem_limit_bytes=16 * 1024 * 1024),
        cost_estimate=pl.CostEstimate(
            flops=EMBED_COST,
            bytes_accessed=0,
            transcendentals=0,
        ),
        name="embed",
    )(fields, affine, weight, other)


def roll_matrix(columns, shift, scale):
    slots = columns // WW * PAD
    row = lax.broadcasted_iota(jnp.int32, (slots, columns), 0)
    column = lax.broadcasted_iota(jnp.int32, (slots, columns), 1)
    place = row % PAD
    want = (row // PAD) * WW + place + shift
    want = jnp.where(want >= columns, want - columns, want)
    hit = (want == column) & (place < WW)
    return jnp.where(hit, scale, 0.0).astype(BF16)


def project_kernel(
    column_offset_ref,
    rows_ref,
    weight_ref,
    other_ref,
    query_ref,
    key_value_ref,
    matrix_ref,
    query_matrix_ref,
):
    rows, columns, features = rows_ref.shape
    width = query_ref.shape[-1]
    shift = column_offset_ref[position()["lon"]]
    refs = weight_ref, other_ref
    collect(parts(refs, 0, LINES, 2 * LINES), matrix_ref)
    for spot, block in parts(refs, LINES, LINES, 2 * LINES):
        block = block.astype(F32)[:, LINES // 2 :]
        block = jnp.concatenate([block[..., :width], block[..., width:]], axis=1)
        collect([(spot, block.reshape(-1, width).astype(BF16))], query_matrix_ref)
    matrix = jnp.concatenate([query_matrix_ref[...], matrix_ref[...]], axis=1)
    to_windows = roll_matrix(columns, shift, 1.0)
    to_queries = roll_matrix(columns, shift, HEAD_DIM**-0.5)
    for row in range(rows):
        normed = layer_norm(rows_ref[row].astype(F32))
        projected = dot(normed, matrix).astype(BF16)
        query_ref[row] = dot(to_queries, projected[:, :width]).astype(BF16)
        key_value_ref[row] = dot(to_windows, projected[:, width:]).astype(BF16)


def project(column_offset, rows_tokens, weights):
    rows, columns, features = rows_tokens.shape
    width = HEADS * HEAD_DIM
    slots = columns // WW * PAD
    return pl.pallas_call(
        project_kernel,
        in_specs=[pl.BlockSpec(memory_space=pltpu.SMEM)]
        + [pl.BlockSpec(memory_space=pltpu.VMEM)] * 3,
        out_shape=[
            jax.ShapeDtypeStruct((rows, slots, width), BF16),
            jax.ShapeDtypeStruct((rows, slots, 2 * width), BF16),
            jax.ShapeDtypeStruct((features, 2 * width), BF16),
        ],
        scratch_shapes=[pltpu.VMEM((features, width), BF16)],
        compiler_params=pltpu.CompilerParams(vmem_limit_bytes=20 * 1024 * 1024),
        cost_estimate=pl.CostEstimate(
            flops=2 * rows * columns * (features + slots) * 3 * width,
            bytes_accessed=rows * columns * features * 2 + rows * slots * 3 * width * 2,
            transcendentals=0,
        ),
        name="project",
    )(column_offset, rows_tokens, *weights)


def choose_kernel(row_offset_ref, north_ref, south_ref, normed_ref):
    rows = normed_ref.shape[0]
    split = row_offset_ref[position()["lon"]]
    for slot in range(rows):
        north = north_ref[jnp.minimum(split - 1 + slot, HALO - 1)]
        south = south_ref[jnp.maximum(slot - (rows - split), 0)]
        values = jnp.where(slot < rows - split, north.astype(F32), south.astype(F32))
        normed_ref[slot] = layer_norm(values)


def choose(row_offset, north, south):
    columns, features = north.shape[1:]
    vmem = pl.BlockSpec(memory_space=pltpu.VMEM)
    return pl.pallas_call(
        choose_kernel,
        in_specs=[pl.BlockSpec(memory_space=pltpu.SMEM), vmem, vmem],
        out_shape=jax.ShapeDtypeStruct((WH, columns, features), BF16),
        compiler_params=pltpu.CompilerParams(vmem_limit_bytes=8 * 1024 * 1024),
        cost_estimate=pl.CostEstimate(flops=CHOOSE_COST, bytes_accessed=0, transcendentals=0),
        name="choose",
    )(row_offset, north, south)


def attend_kernel(
    row_offset_ref,
    column_offset_ref,
    normed_ref,
    query_ref,
    own_ref,
    matrix_ref,
    mixed_ref,
    keys_ref,
    made_ref,
):
    rows, slots, width = query_ref.shape
    columns = normed_ref.shape[1]
    windows = slots // PAD
    here = position()
    lat, last = here["lat"], here["last"]
    split, shift = row_offset_ref[here["lon"]], column_offset_ref[here["lon"]]
    half = keys_ref.shape[0] // 2
    for band in range(2):
        for slot in range(rows, half):
            keys_ref[band * half + slot] = jnp.zeros(keys_ref.shape[1:], BF16)
    for row in range(rows):
        spot = jnp.where(row < split, row + rows - split, half + row - split)
        keys_ref[spot] = own_ref[row]

    matrix = matrix_ref[...]
    to_windows = roll_matrix(columns, shift, 1.0)
    for slot in range(rows):
        projected = dot(normed_ref[slot], matrix).astype(BF16)
        spot = jnp.where(slot < rows - split, slot, half + slot)
        keys_ref[spot] = dot(to_windows, projected).astype(BF16)

    shape = (rows, PAD, half * PAD)
    north_query = lax.broadcasted_iota(jnp.int32, shape, 0) < split
    key = lax.broadcasted_iota(jnp.int32, shape, 2)
    key_row = key // PAD
    from_north = key_row < rows - split
    beyond = jnp.where(
        north_query, jnp.where(from_north, lat, 1), jnp.where(from_north, 1, last - lat)
    )
    bias = jnp.where((key_row < rows) & (key % PAD < WW) & (beyond > 0), 0.0, -1e30)
    lane_head = lax.broadcasted_iota(jnp.int32, (rows * PAD, width), 1) // HEAD_DIM

    def window(m):
        here = pl.ds(pl.multiple_of(m * PAD, PAD), PAD)
        queries = query_ref[:, here, :].reshape(rows * PAD, width)
        keys = keys_ref[:, here, :].reshape(2 * half * PAD, 2 * width)
        zero = jnp.zeros_like(queries)
        stacked = jnp.concatenate(
            [jnp.where(lane_head == head, queries, zero) for head in range(HEADS)], axis=0
        )
        scores = dot_nt(stacked, keys[:, :width]).reshape(HEADS, rows, PAD, 2 * half * PAD)
        scores = jnp.where(north_query[None], scores[..., : half * PAD], scores[..., half * PAD :])
        scores = scores + bias[None]
        weights = jnp.exp(scores - jnp.max(scores, axis=-1, keepdims=True))
        weights = weights * (1.0 / jnp.sum(weights, axis=-1, keepdims=True))
        weights = jnp.concatenate(
            [jnp.where(north_query[None], weights, 0.0), jnp.where(north_query[None], 0.0, weights)],
            axis=-1,
        ).astype(BF16)
        products = dot(weights.reshape(HEADS * rows * PAD, -1), keys[:, width:])
        products = products.reshape(HEADS, rows * PAD, width)
        mixed = products[0]
        for head in range(1, HEADS):
            mixed = jnp.where(lane_head == head, products[head], mixed)
        mixed = mixed.astype(BF16).reshape(rows, PAD, width)
        made_ref[:, pl.ds(pl.multiple_of((m + 1) * PAD, PAD), PAD), :] = mixed

    def some_windows(step, carry):
        for inner in range(GROUP):
            window(step * GROUP + inner)
        return carry

    lax.fori_loop(0, windows // GROUP, some_windows, 0)
    made_ref[:, :PAD, :] = made_ref[:, windows * PAD :, :]

    def source(k):
        row, column = k // WW, k % WW
        inner = jnp.where(column < shift, column + WW - shift, PAD + column - shift)
        return row * (2 * PAD) + inner

    back = one_hot((rows * WW, rows * 2 * PAD), source)
    for j in range(windows):
        pair = made_ref[:, j * PAD : (j + 2) * PAD, :]
        mixed_ref[j] = dot(back, pair.reshape(rows * 2 * PAD, width)).astype(BF16)


def attend(row_offset, column_offset, normed, queries, own, matrix):
    rows, slots, width = queries.shape
    windows = slots // PAD
    columns, features = normed.shape[1:]
    vmem = pl.BlockSpec(memory_space=pltpu.VMEM)
    return pl.pallas_call(
        attend_kernel,
        in_specs=[pl.BlockSpec(memory_space=pltpu.SMEM)] * 2 + [vmem] * 4,
        out_shape=jax.ShapeDtypeStruct((windows, rows * WW, width), BF16),
        scratch_shapes=[
            pltpu.VMEM((2 * BAND, slots, 2 * width), BF16),
            pltpu.VMEM((rows, slots + PAD, width), BF16),
        ],
        compiler_params=pltpu.CompilerParams(vmem_limit_bytes=24 * 1024 * 1024),
        cost_estimate=pl.CostEstimate(
            flops=ATTEND_COST * 2 * rows * columns * (features + slots) * 2 * width
            + ATTEND_COST * 4 * windows * HEADS * rows * PAD * 2 * rows * PAD * width,
            bytes_accessed=normed.size * 2 + rows * slots * 4 * width * 2,
            transcendentals=windows * HEADS * rows * PAD * 2 * rows * PAD,
        ),
        name="attend",
    )(row_offset, column_offset, normed, queries, own, matrix)


def finish_kernel(
    tokens_ref,
    mixed_ref,
    first_own_ref,
    first_other_ref,
    second_own_ref,
    second_other_ref,
    near_ref,
    near_other_ref,
    encoded_ref,
    out_ref,
    first_ref,
    second_ref,
):
    count, cells, features = tokens_ref.shape
    lines = LINES

    @pl.when(pl.program_id(0) == 0)
    def _():
        refs = first_own_ref, first_other_ref
        collect(parts(refs, 0, lines, 2 * lines), first_ref, slice(0, features))
        collect(parts(refs, lines, lines, 2 * lines), first_ref, slice(features, 2 * features))
        refs = second_own_ref, second_other_ref
        collect(parts(refs, 0, 2 * lines, 2 * lines), second_ref)
        for spot, block in parts((near_ref, near_other_ref), lines, lines, 2 * lines):
            block = block.astype(F32)[:, : lines // 2].reshape(-1, features)
            collect([(spot, block.astype(BF16))], out_ref)

    tokens = tokens_ref[...].astype(F32).reshape(count * cells, features)
    mixed = mixed_ref[...].astype(F32).reshape(count * cells, -1).astype(BF16)
    residual = tokens + dot(mixed, out_ref[...])
    inner = layer_norm(residual)
    expanded = jax.nn.gelu(dot(inner, first_ref[...]), approximate=True).astype(BF16)
    encoded = (residual + dot(expanded, second_ref[...])).astype(BF16)
    size = count * cells
    order = one_hot((size, size), lambda k: (k % count) * cells + k // count)
    encoded_ref[...] = dot(order, encoded).astype(BF16).reshape(cells, count, features)


def finish(tokens, mixed, weights):
    count, cells, features = tokens.shape
    width = mixed.shape[2]
    hidden = 2 * features
    block = 24
    return pl.pallas_call(
        finish_kernel,
        grid=(cells // block,),
        in_specs=[
            pl.BlockSpec((count, block, features), lambda g: (0, g, 0)),
            pl.BlockSpec((count, block, width), lambda g: (0, g, 0)),
        ]
        + [pl.BlockSpec(weight.shape, lambda g: (0, 0, 0)) for weight in weights],
        out_specs=pl.BlockSpec((block, count, features), lambda g: (g, 0, 0)),
        out_shape=jax.ShapeDtypeStruct((cells, count, features), BF16),
        scratch_shapes=[
            pltpu.VMEM((width, features), BF16),
            pltpu.VMEM((features, hidden), BF16),
            pltpu.VMEM((hidden, features), BF16),
        ],
        compiler_params=pltpu.CompilerParams(vmem_limit_bytes=24 * 1024 * 1024),
        cost_estimate=pl.CostEstimate(
            flops=2 * count * cells * features * (width + 2 * hidden),
            bytes_accessed=count * cells * (4 * features + 2 * width) + weights[0].size * 12,
            transcendentals=count * cells * hidden,
        ),
        name="finish",
    )(tokens, mixed, *weights)


def copies(values, count):
    return jnp.broadcast_to(values[None], (count,) + values.shape)


def gather_far(shard):
    sizes = lax.axis_size("y_lo"), lax.axis_size("lat")
    found = lax.all_to_all(copies(shard, sizes[0] * sizes[1]), ("y_lo", "lat"), 0, 0, tiled=True)
    return found.reshape(sizes + shard.shape)


def swap(values, axis):
    return lax.ppermute(values, axis, [(0, 1), (1, 0)])


def after(first, *later):
    return lax.optimization_barrier((first,) + later)


def shards(
    fields,
    scale_exponent,
    level_mean,
    level_spread,
    row_offset,
    column_offset,
    patch_weight,
    attention_in,
    attention_out,
    hidden_in,
    hidden_out,
):
    features = patch_weight.shape[1]
    chans = fields.shape[3]
    lats = lax.axis_size("lat")
    repeat = chans // level_mean.shape[0]
    affine = jnp.stack(
        [
            jnp.tile(jnp.exp2(scale_exponent.astype(F32)) / level_spread, repeat),
            jnp.tile(level_mean / level_spread, repeat),
        ]
    )

    packed = pack(hidden_in, hidden_out, attention_out, attention_in)
    early, late = join(packed, swap(packed, "y_lo"))
    early = lax.all_gather(early, "lat", axis=0)
    patch = gather_far(patch_weight)

    rows_tokens, top, bottom, tiles = embed(fields[0], affine, patch, swap(patch, "core"))
    _, early = after(rows_tokens, early)
    _, late = after(rows_tokens, late)
    late = lax.all_gather(late, "lat", axis=0)
    north = lax.ppermute(bottom, "lat", [(i, i + 1) for i in range(lats - 1)])
    south = lax.ppermute(top, "lat", [(i + 1, i) for i in range(lats - 1)])
    tiles = tiles.reshape(-1, WH * WW, features)
    tile_tokens = lax.all_to_all(tiles, ("y_hi", "x"), 0, 0, tiled=True)

    half = 4 * LINES
    near = early[:, :half]
    near = near, swap(near, "core")
    window_queries, own, matrix = project(column_offset, rows_tokens, near)
    normed = choose(row_offset, north, south)
    mixed = attend(row_offset, column_offset, normed, window_queries, own, matrix)
    _, mixed = after(tile_tokens, mixed)
    _, first, second = after(mixed, early[:, half:], late[:, :half])
    tile_mixed = lax.all_to_all(mixed, ("y_hi", "x"), 0, 0, tiled=True)
    weights = (first, swap(first, "core"), second, swap(second, "core")) + near
    encoded = finish(tile_tokens, tile_mixed, weights)
    return encoded.reshape(WH, WW, -1, features).transpose(2, 0, 1, 3)


def solution(mesh):
    tm, lat, lon = (mesh.shape[name] for name in ("tm", "lat", "lon"))
    cores, across = 2, 4
    finer = Mesh(
        mesh.devices.reshape(tm // cores, cores, lat, lon // across, across),
        ("y_lo", "core", "lat", "y_hi", "x"),
    )
    time = ("y_lo", "core")
    in_specs = (
        P(time + ("y_hi", "x"), "lat", None, None),
        P(),
        P(),
        P(),
        P(time),
        P(time),
        P(time + ("lat",), None),
        P(time + ("lat",), None),
        P(time + ("lat",), None),
        P(time + ("lat",), None),
        P(time + ("lat",), None),
    )
    out_specs = P(time, "lat", ("y_hi", "x"), None)
    return jax.shard_map(shards, mesh=finer, in_specs=in_specs, out_specs=out_specs, check_vma=False)
```

```python
import functools

import jax
import jax.numpy as jnp
from jax import lax
from jax.experimental import pallas as pl
from jax.experimental.pallas import tpu as pltpu
from jax.sharding import Mesh
from jax.sharding import PartitionSpec as P

P_SIZE = 4
HEAD_DIM = 64
HEADS = 4
WH = 6
WW = 12
PAD = 16
HALO = WH - 1
BAND = 8
EPSILON = 1e-05
BF16 = jnp.bfloat16
F32 = jnp.float32
GROUP = 4
ATTEND_COST = 1
EMBED_COST = 3 * 10**9
CHOOSE_COST = 3 * 10**10
LINES = 16


def dot(a, b):
    return jnp.dot(a, b, preferred_element_type=F32)


def dot_nt(a, b):
    return lax.dot_general(a, b, (((1,), (1,)), ((), ())), preferred_element_type=F32)


def one_hot(shape, column_of_row):
    row = lax.broadcasted_iota(jnp.int32, (shape[0], 1), 0)
    column = lax.broadcasted_iota(jnp.int32, shape, 1)
    return jnp.where(column == column_of_row(row), 1.0, 0.0).astype(BF16)


def layer_norm(values):
    center = values - jnp.mean(values, axis=-1, keepdims=True)
    spread = jnp.mean(center * center, axis=-1, keepdims=True)
    return (center * lax.rsqrt(spread + EPSILON)).astype(BF16)


def position():
    lon = lax.axis_index("y_hi") * lax.axis_size("x") + lax.axis_index("x")
    return {
        "core": lax.axis_index("core"),
        "y_lo": lax.axis_index("y_lo"),
        "lat": lax.axis_index("lat"),
        "last": lax.axis_size("lat") - 1,
        "lon": lon,
    }


def place(core_swapped, y_swapped):
    here = position()
    core, y = here["core"], here["y_lo"]
    core = 1 - core if core_swapped else core
    y = 1 - y if y_swapped else y
    return y * 2 + core


def collect(shards, target_ref, columns=slice(None)):
    for spot, block in shards:
        block = block.reshape(-1, block.shape[-1])
        start = pl.multiple_of(spot * block.shape[0], block.shape[0])
        target_ref[pl.ds(start, block.shape[0]), columns] = block


def parts(refs, first, count, half):
    return [
        (place(swapped, y), ref[:, y * half + first : y * half + first + count])
        for swapped, ref in enumerate(refs)
        for y in range(2)
    ]


def pack_kernel(
    patch_ref, hidden_in_ref, hidden_out_ref, attention_out_ref, attention_in_ref, copies_ref, packed_ref
):
    for k in range(copies_ref.shape[0]):
        copies_ref[k] = patch_ref[...]
    lines, features = LINES, packed_ref.shape[1]
    short = lines // 2
    width = attention_in_ref.shape[1] // 3
    packed_ref[:lines] = hidden_in_ref[:, :features]
    packed_ref[lines : 2 * lines] = hidden_in_ref[:, features:]
    packed_ref[2 * lines : 4 * lines] = hidden_out_ref[...]
    packed_ref[4 * lines : 5 * lines] = attention_in_ref[:, width:]
    query = attention_in_ref[:, :width].astype(F32)
    query = jnp.concatenate([query[:short], query[short:]], axis=1)
    out = attention_out_ref[...].astype(F32)
    packed_ref[5 * lines :] = jnp.concatenate([out, query], axis=0).astype(BF16)


def pack(count, patch, hidden_in, hidden_out, attention_out, attention_in):
    return pl.pallas_call(
        pack_kernel,
        in_specs=[pl.BlockSpec(memory_space=pltpu.VMEM)] * 5,
        out_shape=[
            jax.ShapeDtypeStruct((count,) + patch.shape, BF16),
            jax.ShapeDtypeStruct((6 * LINES, hidden_out.shape[1]), BF16),
        ],
        name="pack",
    )(patch, hidden_in, hidden_out, attention_out, attention_in)


def join_kernel(own_ref, swapped_ref, joined_ref):
    far = 4 * LINES
    near = own_ref.shape[0] - far
    joined_ref[:far] = own_ref[:far]
    joined_ref[far : 2 * far] = swapped_ref[:far]
    joined_ref[2 * far : 2 * far + near] = own_ref[far:]
    joined_ref[2 * far + near :] = swapped_ref[far:]


def join(own, swapped):
    return pl.pallas_call(
        join_kernel,
        in_specs=[pl.BlockSpec(memory_space=pltpu.VMEM)] * 2,
        out_shape=jax.ShapeDtypeStruct((2 * own.shape[0], own.shape[1]), BF16),
        name="join",
    )(own, swapped)


def embed_kernel(
    fields_ref,
    affine_ref,
    weight_ref,
    other_ref,
    rows_ref,
    top_ref,
    bottom_ref,
    tiles_ref,
    table_ref,
    order_ref,
):
    rows = rows_ref.shape[0]
    columns = fields_ref.shape[1]

    def source(k):
        tile, inner = k // (rows * WW), k % (rows * WW)
        return (inner // WW) * columns + tile * WW + inner % WW

    @pl.when(pl.program_id(0) == 0)
    def _():
        for swapped, ref in enumerate((weight_ref, other_ref)):
            for y in range(ref.shape[0]):
                core = place(swapped, 0) % 2
                table_ref[2 * y + core] = ref[y].reshape(table_ref.shape[1:])
        order_ref[...] = one_hot(order_ref.shape, source)

    chans = fields_ref.shape[2]
    raw = fields_ref[...].reshape(rows, P_SIZE, columns, chans)
    factor = affine_ref[0:1, :]
    shift = affine_ref[1:2, :]
    total = None
    for pixel in range(P_SIZE):
        part = raw[:, pixel].reshape(rows * columns, chans).astype(F32)
        part = (part * factor - shift).astype(BF16)
        product = dot(part, table_ref[pixel])
        total = product if total is None else total + product
    tokens = total.astype(BF16)
    by_row = tokens.reshape(rows, columns, -1)
    rows_ref[...] = by_row
    top_ref[...] = by_row[:HALO]
    bottom_ref[...] = by_row[rows - HALO :]

    tiles_ref[...] = dot(order_ref[...], tokens).astype(BF16)


def embed(fields, affine, weight, other):
    pixel_rows, columns, chans = fields.shape
    rows = pixel_rows // P_SIZE
    width = weight.shape[-1]
    step = GROUP * WW
    return pl.pallas_call(
        embed_kernel,
        grid=(columns // step,),
        in_specs=[
            pl.BlockSpec((pixel_rows, step, chans), lambda g: (0, g, 0)),
            pl.BlockSpec(affine.shape, lambda g: (0, 0)),
            pl.BlockSpec(weight.shape, lambda g: (0,) * weight.ndim),
            pl.BlockSpec(weight.shape, lambda g: (0,) * weight.ndim),
        ],
        out_specs=[
            pl.BlockSpec((rows, step, width), lambda g: (0, g, 0)),
            pl.BlockSpec((HALO, step, width), lambda g: (0, g, 0)),
            pl.BlockSpec((HALO, step, width), lambda g: (0, g, 0)),
            pl.BlockSpec((rows * step, width), lambda g: (g, 0)),
        ],
        out_shape=[
            jax.ShapeDtypeStruct((rows, columns, width), BF16),
            jax.ShapeDtypeStruct((HALO, columns, width), BF16),
            jax.ShapeDtypeStruct((HALO, columns, width), BF16),
            jax.ShapeDtypeStruct((rows * columns, width), BF16),
        ],
        scratch_shapes=[
            pltpu.VMEM((P_SIZE, chans, width), BF16),
            pltpu.VMEM((rows * step, rows * step), BF16),
        ],
        compiler_params=pltpu.CompilerParams(vmem_limit_bytes=16 * 1024 * 1024),
        cost_estimate=pl.CostEstimate(
            flops=EMBED_COST,
            bytes_accessed=0,
            transcendentals=0,
        ),
        name="embed",
    )(fields, affine, weight, other)


def roll_matrix(columns, shift, scale):
    slots = columns // WW * PAD
    row = lax.broadcasted_iota(jnp.int32, (slots, 1), 0)
    column = lax.broadcasted_iota(jnp.int32, (slots, columns), 1)
    place = row % PAD
    want = (row // PAD) * WW + place + shift
    want = jnp.where(want >= columns, want - columns, want)
    want = jnp.where(place < WW, want, columns)
    return jnp.where(column == want, scale, 0.0).astype(BF16)


def project_kernel(
    column_offset_ref,
    rows_ref,
    weight_ref,
    other_ref,
    query_ref,
    key_value_ref,
    matrix_ref,
    query_matrix_ref,
):
    rows, columns, features = rows_ref.shape
    width = query_ref.shape[-1]
    shift = column_offset_ref[position()["lon"]]
    refs = weight_ref, other_ref
    collect(parts(refs, 0, LINES, 2 * LINES), matrix_ref)
    for spot, block in parts(refs, LINES, LINES, 2 * LINES):
        block = block.astype(F32)[:, LINES // 2 :]
        block = jnp.concatenate([block[..., :width], block[..., width:]], axis=1)
        collect([(spot, block.reshape(-1, width).astype(BF16))], query_matrix_ref)
    matrix = jnp.concatenate([query_matrix_ref[...], matrix_ref[...]], axis=1)
    to_windows = roll_matrix(columns, shift, 1.0)
    to_queries = roll_matrix(columns, shift, HEAD_DIM**-0.5)
    for row in range(rows):
        normed = layer_norm(rows_ref[row].astype(F32))
        projected = dot(normed, matrix).astype(BF16)
        query_ref[row] = dot(to_queries, projected[:, :width]).astype(BF16)
        key_value_ref[row] = dot(to_windows, projected[:, width:]).astype(BF16)


def project(column_offset, rows_tokens, weights):
    rows, columns, features = rows_tokens.shape
    width = HEADS * HEAD_DIM
    slots = columns // WW * PAD
    return pl.pallas_call(
        project_kernel,
        in_specs=[pl.BlockSpec(memory_space=pltpu.SMEM)]
        + [pl.BlockSpec(memory_space=pltpu.VMEM)] * 3,
        out_shape=[
            jax.ShapeDtypeStruct((rows, slots, width), BF16),
            jax.ShapeDtypeStruct((rows, slots, 2 * width), BF16),
            jax.ShapeDtypeStruct((features, 2 * width), BF16),
        ],
        scratch_shapes=[pltpu.VMEM((features, width), BF16)],
        compiler_params=pltpu.CompilerParams(vmem_limit_bytes=20 * 1024 * 1024),
        cost_estimate=pl.CostEstimate(
            flops=2 * rows * columns * (features + slots) * 3 * width,
            bytes_accessed=rows * columns * features * 2 + rows * slots * 3 * width * 2,
            transcendentals=0,
        ),
        name="project",
    )(column_offset, rows_tokens, *weights)


def choose_kernel(row_offset_ref, north_ref, south_ref, normed_ref):
    rows = normed_ref.shape[0]
    split = row_offset_ref[position()["lon"]]
    for slot in range(rows):
        north = north_ref[jnp.minimum(split - 1 + slot, HALO - 1)]
        south = south_ref[jnp.maximum(slot - (rows - split), 0)]
        values = jnp.where(slot < rows - split, north.astype(F32), south.astype(F32))
        normed_ref[slot] = layer_norm(values)


def choose(row_offset, north, south):
    columns, features = north.shape[1:]
    vmem = pl.BlockSpec(memory_space=pltpu.VMEM)
    return pl.pallas_call(
        choose_kernel,
        in_specs=[pl.BlockSpec(memory_space=pltpu.SMEM), vmem, vmem],
        out_shape=jax.ShapeDtypeStruct((WH, columns, features), BF16),
        compiler_params=pltpu.CompilerParams(vmem_limit_bytes=8 * 1024 * 1024),
        cost_estimate=pl.CostEstimate(flops=CHOOSE_COST, bytes_accessed=0, transcendentals=0),
        name="choose",
    )(row_offset, north, south)


def attend_kernel(
    row_offset_ref,
    column_offset_ref,
    normed_ref,
    query_ref,
    own_ref,
    matrix_ref,
    mixed_ref,
    keys_ref,
    made_ref,
):
    rows, slots, width = query_ref.shape
    columns = normed_ref.shape[1]
    windows = slots // PAD
    here = position()
    lat, last = here["lat"], here["last"]
    split, shift = row_offset_ref[here["lon"]], column_offset_ref[here["lon"]]
    half = keys_ref.shape[0] // 2
    for band in range(2):
        for slot in range(rows, half):
            keys_ref[band * half + slot] = jnp.zeros(keys_ref.shape[1:], BF16)
    for row in range(rows):
        spot = jnp.where(row < split, row + rows - split, half + row - split)
        keys_ref[spot] = own_ref[row]

    matrix = matrix_ref[...]
    to_windows = roll_matrix(columns, shift, 1.0)
    for slot in range(rows):
        projected = dot(normed_ref[slot], matrix).astype(BF16)
        spot = jnp.where(slot < rows - split, slot, half + slot)
        keys_ref[spot] = dot(to_windows, projected).astype(BF16)

    shape = (rows, PAD, half * PAD)
    north_query = lax.broadcasted_iota(jnp.int32, shape, 0) < split
    key = lax.broadcasted_iota(jnp.int32, shape, 2)
    key_row = key // PAD
    from_north = key_row < rows - split
    beyond = jnp.where(
        north_query, jnp.where(from_north, lat, 1), jnp.where(from_north, 1, last - lat)
    )
    bias = jnp.where((key_row < rows) & (key % PAD < WW) & (beyond > 0), 0.0, -1e30)
    lane_head = lax.broadcasted_iota(jnp.int32, (rows * PAD, width), 1) // HEAD_DIM

    def window(m):
        here = pl.ds(pl.multiple_of(m * PAD, PAD), PAD)
        queries = query_ref[:, here, :].reshape(rows * PAD, width)
        keys = keys_ref[:, here, :].reshape(2 * half * PAD, 2 * width)
        zero = jnp.zeros_like(queries)
        stacked = jnp.concatenate(
            [jnp.where(lane_head == head, queries, zero) for head in range(HEADS)], axis=0
        )
        scores = dot_nt(stacked, keys[:, :width]).reshape(HEADS, rows, PAD, 2 * half * PAD)
        scores = jnp.where(north_query[None], scores[..., : half * PAD], scores[..., half * PAD :])
        scores = scores + bias[None]
        weights = jnp.exp(scores - jnp.max(scores, axis=-1, keepdims=True))
        weights = weights * (1.0 / jnp.sum(weights, axis=-1, keepdims=True))
        weights = jnp.concatenate(
            [jnp.where(north_query[None], weights, 0.0), jnp.where(north_query[None], 0.0, weights)],
            axis=-1,
        ).astype(BF16)
        products = dot(weights.reshape(HEADS * rows * PAD, -1), keys[:, width:])
        products = products.reshape(HEADS, rows * PAD, width)
        mixed = products[0]
        for head in range(1, HEADS):
            mixed = jnp.where(lane_head == head, products[head], mixed)
        mixed = mixed.astype(BF16).reshape(rows, PAD, width)
        made_ref[:, pl.ds(pl.multiple_of((m + 1) * PAD, PAD), PAD), :] = mixed

    def some_windows(step, carry):
        for inner in range(GROUP):
            window(step * GROUP + inner)
        return carry

    lax.fori_loop(0, windows // GROUP, some_windows, 0)
    made_ref[:, :PAD, :] = made_ref[:, windows * PAD :, :]

    def source(k):
        row, column = k // WW, k % WW
        inner = jnp.where(column < shift, column + WW - shift, PAD + column - shift)
        return row * (2 * PAD) + inner

    back = one_hot((rows * WW, rows * 2 * PAD), source)
    for j in range(windows):
        pair = made_ref[:, j * PAD : (j + 2) * PAD, :]
        mixed_ref[j] = dot(back, pair.reshape(rows * 2 * PAD, width)).astype(BF16)


def attend(row_offset, column_offset, normed, queries, own, matrix):
    rows, slots, width = queries.shape
    windows = slots // PAD
    columns, features = normed.shape[1:]
    vmem = pl.BlockSpec(memory_space=pltpu.VMEM)
    return pl.pallas_call(
        attend_kernel,
        in_specs=[pl.BlockSpec(memory_space=pltpu.SMEM)] * 2 + [vmem] * 4,
        out_shape=jax.ShapeDtypeStruct((windows, rows * WW, width), BF16),
        scratch_shapes=[
            pltpu.VMEM((2 * BAND, slots, 2 * width), BF16),
            pltpu.VMEM((rows, slots + PAD, width), BF16),
        ],
        compiler_params=pltpu.CompilerParams(vmem_limit_bytes=24 * 1024 * 1024),
        cost_estimate=pl.CostEstimate(
            flops=ATTEND_COST * 2 * rows * columns * (features + slots) * 2 * width
            + ATTEND_COST * 4 * windows * HEADS * rows * PAD * 2 * rows * PAD * width,
            bytes_accessed=normed.size * 2 + rows * slots * 4 * width * 2,
            transcendentals=windows * HEADS * rows * PAD * 2 * rows * PAD,
        ),
        name="attend",
    )(row_offset, column_offset, normed, queries, own, matrix)


def finish_kernel(
    tokens_ref,
    mixed_ref,
    hidden_ref,
    hidden_other_ref,
    near_ref,
    near_other_ref,
    encoded_ref,
    out_ref,
    first_ref,
    second_ref,
    order_ref,
):
    count, cells, features = tokens_ref.shape
    lines = LINES

    @pl.when(pl.program_id(0) == 0)
    def _():
        refs = hidden_ref, hidden_other_ref
        collect(parts(refs, 0, lines, 4 * lines), first_ref, slice(0, features))
        collect(parts(refs, lines, lines, 4 * lines), first_ref, slice(features, 2 * features))
        collect(parts(refs, 2 * lines, 2 * lines, 4 * lines), second_ref)
        for spot, block in parts((near_ref, near_other_ref), lines, lines, 2 * lines):
            block = block.astype(F32)[:, : lines // 2].reshape(-1, features)
            collect([(spot, block.astype(BF16))], out_ref)
        order_ref[...] = one_hot(order_ref.shape, lambda k: (k % count) * cells + k // count)

    tokens = tokens_ref[...].astype(F32).reshape(count * cells, features)
    mixed = mixed_ref[...].astype(F32).reshape(count * cells, -1).astype(BF16)
    residual = tokens + dot(mixed, out_ref[...])
    inner = layer_norm(residual)
    expanded = jax.nn.gelu(dot(inner, first_ref[...]), approximate=True).astype(BF16)
    encoded = (residual + dot(expanded, second_ref[...])).astype(BF16)
    encoded_ref[...] = dot(order_ref[...], encoded).astype(BF16).reshape(cells, count, features)


def finish(tokens, mixed, weights):
    count, cells, features = tokens.shape
    width = mixed.shape[2]
    hidden = 2 * features
    block = 24
    return pl.pallas_call(
        finish_kernel,
        grid=(cells // block,),
        in_specs=[
            pl.BlockSpec((count, block, features), lambda g: (0, g, 0)),
            pl.BlockSpec((count, block, width), lambda g: (0, g, 0)),
        ]
        + [pl.BlockSpec(weight.shape, lambda g: (0, 0, 0)) for weight in weights],
        out_specs=pl.BlockSpec((block, count, features), lambda g: (g, 0, 0)),
        out_shape=jax.ShapeDtypeStruct((cells, count, features), BF16),
        scratch_shapes=[
            pltpu.VMEM((width, features), BF16),
            pltpu.VMEM((features, hidden), BF16),
            pltpu.VMEM((hidden, features), BF16),
            pltpu.VMEM((count * block, count * block), BF16),
        ],
        compiler_params=pltpu.CompilerParams(vmem_limit_bytes=24 * 1024 * 1024),
        cost_estimate=pl.CostEstimate(
            flops=2 * count * cells * features * (width + 2 * hidden),
            bytes_accessed=count * cells * (4 * features + 2 * width) + weights[0].size * 6,
            transcendentals=count * cells * hidden,
        ),
        name="finish",
    )(tokens, mixed, *weights)


def swap(values, axis):
    return lax.ppermute(values, axis, [(0, 1), (1, 0)])


def after(first, *later):
    return lax.optimization_barrier((first,) + later)


def shards(
    fields,
    scale_exponent,
    level_mean,
    level_spread,
    row_offset,
    column_offset,
    patch_weight,
    attention_in,
    attention_out,
    hidden_in,
    hidden_out,
):
    features = patch_weight.shape[1]
    chans = fields.shape[3]
    lats = lax.axis_size("lat")
    repeat = chans // level_mean.shape[0]
    affine = jnp.stack(
        [
            jnp.tile(jnp.exp2(scale_exponent.astype(F32)) / level_spread, repeat),
            jnp.tile(level_mean / level_spread, repeat),
        ]
    )

    far = lax.axis_size("y_lo"), lats
    patch, packed = pack(
        far[0] * far[1], patch_weight, hidden_in, hidden_out, attention_out, attention_in
    )
    packed = join(packed, swap(packed, "y_lo"))
    rest = lax.all_gather(packed, "lat", axis=0)
    patch = lax.all_to_all(patch, ("y_lo", "lat"), 0, 0, tiled=True)
    patch = patch.reshape(far + patch_weight.shape)

    rows_tokens, top, bottom, tiles = embed(fields[0], affine, patch, swap(patch, "core"))
    _, rest = after(rows_tokens, rest)
    north = lax.ppermute(bottom, "lat", [(i, i + 1) for i in range(lats - 1)])
    south = lax.ppermute(top, "lat", [(i + 1, i) for i in range(lats - 1)])
    tiles = tiles.reshape(-1, WH * WW, features)
    tile_tokens = lax.all_to_all(tiles, ("y_hi", "x"), 0, 0, tiled=True)

    near = rest[:, 8 * LINES :]
    near = near, swap(near, "core")
    window_queries, own, matrix = project(column_offset, rows_tokens, near)
    normed = choose(row_offset, north, south)
    mixed = attend(row_offset, column_offset, normed, window_queries, own, matrix)
    _, mixed = after(tile_tokens, mixed)
    _, hidden_weight = after(mixed, rest[:, : 8 * LINES])
    tile_mixed = lax.all_to_all(mixed, ("y_hi", "x"), 0, 0, tiled=True)
    encoded = finish(tile_tokens, tile_mixed, (hidden_weight, swap(hidden_weight, "core")) + near)
    return encoded.reshape(WH, WW, -1, features).transpose(2, 0, 1, 3)


def solution(mesh):
    tm, lat, lon = (mesh.shape[name] for name in ("tm", "lat", "lon"))
    cores, across = 2, 4
    finer = Mesh(
        mesh.devices.reshape(tm // cores, cores, lat, lon // across, across),
        ("y_lo", "core", "lat", "y_hi", "x"),
    )
    time = ("y_lo", "core")
    in_specs = (
        P(time + ("y_hi", "x"), "lat", None, None),
        P(),
        P(),
        P(),
        P(time),
        P(time),
        P(time + ("lat",), None),
        P(time + ("lat",), None),
        P(time + ("lat",), None),
        P(time + ("lat",), None),
        P(time + ("lat",), None),
    )
    out_specs = P(time, "lat", ("y_hi", "x"), None)
    return jax.shard_map(shards, mesh=finer, in_specs=in_specs, out_specs=out_specs, check_vma=False)
```

```python
import functools

import jax
import jax.numpy as jnp
from jax import lax
from jax.experimental import pallas as pl
from jax.experimental.pallas import tpu as pltpu
from jax.sharding import Mesh
from jax.sharding import PartitionSpec as P

P_SIZE = 4
HEAD_DIM = 64
HEADS = 4
WH = 6
WW = 12
PAD = 16
HALO = WH - 1
BAND = 8
EPSILON = 1e-05
BF16 = jnp.bfloat16
F32 = jnp.float32
GROUP = 4
ATTEND_COST = 5
EMBED_COST = 8 * 10**9
LINES = 16


def dot(a, b):
    return jnp.dot(a, b, preferred_element_type=F32)


def dot_nt(a, b):
    return lax.dot_general(a, b, (((1,), (1,)), ((), ())), preferred_element_type=F32)


def one_hot(shape, column_of_row):
    row = lax.broadcasted_iota(jnp.int32, (shape[0], 1), 0)
    column = lax.broadcasted_iota(jnp.int32, shape, 1)
    return jnp.where(column == column_of_row(row), 1.0, 0.0).astype(BF16)


def layer_norm(values):
    center = values - jnp.mean(values, axis=-1, keepdims=True)
    spread = jnp.mean(center * center, axis=-1, keepdims=True)
    return (center * lax.rsqrt(spread + EPSILON)).astype(BF16)


def position():
    lon = lax.axis_index("y_hi") * lax.axis_size("x") + lax.axis_index("x")
    return {
        "core": lax.axis_index("core"),
        "y_lo": lax.axis_index("y_lo"),
        "lat": lax.axis_index("lat"),
        "last": lax.axis_size("lat") - 1,
        "lon": lon,
    }


def place(core_swapped, y_swapped):
    here = position()
    core, y = here["core"], here["y_lo"]
    core = 1 - core if core_swapped else core
    y = 1 - y if y_swapped else y
    return y * 2 + core


def collect(shards, target_ref, columns=slice(None)):
    for spot, block in shards:
        block = block.reshape(-1, block.shape[-1])
        start = pl.multiple_of(spot * block.shape[0], block.shape[0])
        target_ref[pl.ds(start, block.shape[0]), columns] = block


def parts(refs, first, count, half):
    return [
        (place(swapped, y), ref[:, y * half + first : y * half + first + count])
        for swapped, ref in enumerate(refs)
        for y in range(2)
    ]


def pack_kernel(
    patch_ref, hidden_in_ref, hidden_out_ref, attention_out_ref, attention_in_ref, copies_ref, packed_ref
):
    for k in range(copies_ref.shape[0]):
        copies_ref[k] = patch_ref[...]
    lines, features = LINES, packed_ref.shape[1]
    short = lines // 2
    width = attention_in_ref.shape[1] // 3
    packed_ref[:lines] = hidden_in_ref[:, :features]
    packed_ref[lines : 2 * lines] = hidden_in_ref[:, features:]
    packed_ref[2 * lines : 4 * lines] = hidden_out_ref[...]
    packed_ref[4 * lines : 5 * lines] = attention_in_ref[:, width:]
    query = attention_in_ref[:, :width].astype(F32)
    query = jnp.concatenate([query[:short], query[short:]], axis=1)
    out = attention_out_ref[...].astype(F32)
    packed_ref[5 * lines :] = jnp.concatenate([out, query], axis=0).astype(BF16)


def pack(count, patch, hidden_in, hidden_out, attention_out, attention_in):
    return pl.pallas_call(
        pack_kernel,
        in_specs=[pl.BlockSpec(memory_space=pltpu.VMEM)] * 5,
        out_shape=[
            jax.ShapeDtypeStruct((count,) + patch.shape, BF16),
            jax.ShapeDtypeStruct((6 * LINES, hidden_out.shape[1]), BF16),
        ],
        name="pack",
    )(patch, hidden_in, hidden_out, attention_out, attention_in)


def join_kernel(own_ref, swapped_ref, joined_ref):
    far = 4 * LINES
    near = own_ref.shape[0] - far
    joined_ref[:far] = own_ref[:far]
    joined_ref[far : 2 * far] = swapped_ref[:far]
    joined_ref[2 * far : 2 * far + near] = own_ref[far:]
    joined_ref[2 * far + near :] = swapped_ref[far:]


def join(own, swapped):
    return pl.pallas_call(
        join_kernel,
        in_specs=[pl.BlockSpec(memory_space=pltpu.VMEM)] * 2,
        out_shape=jax.ShapeDtypeStruct((2 * own.shape[0], own.shape[1]), BF16),
        name="join",
    )(own, swapped)


def embed_kernel(
    fields_ref,
    affine_ref,
    weight_ref,
    other_ref,
    top_ref,
    bottom_ref,
    tiles_ref,
    table_ref,
    order_ref,
):
    rows = fields_ref.shape[0] // P_SIZE
    columns = fields_ref.shape[1]

    def source(k):
        tile, inner = k // (rows * WW), k % (rows * WW)
        return (inner // WW) * columns + tile * WW + inner % WW

    @pl.when(pl.program_id(0) == 0)
    def _():
        for swapped, ref in enumerate((weight_ref, other_ref)):
            for y in range(ref.shape[0]):
                core = place(swapped, 0) % 2
                table_ref[2 * y + core] = ref[y].reshape(table_ref.shape[1:])
        order_ref[...] = one_hot(order_ref.shape, source)

    chans = fields_ref.shape[2]
    raw = fields_ref[...].reshape(rows, P_SIZE, columns, chans)
    factor = affine_ref[0:1, :]
    shift = affine_ref[1:2, :]
    total = None
    for pixel in range(P_SIZE):
        part = raw[:, pixel].reshape(rows * columns, chans).astype(F32)
        part = (part * factor - shift).astype(BF16)
        product = dot(part, table_ref[pixel])
        total = product if total is None else total + product
    tokens = total.astype(BF16)
    by_row = tokens.reshape(rows, columns, -1)
    top_ref[...] = by_row[:HALO]
    bottom_ref[...] = by_row[rows - HALO :]

    tiles_ref[...] = dot(order_ref[...], tokens).astype(BF16)


def embed(fields, affine, weight, other):
    pixel_rows, columns, chans = fields.shape
    rows = pixel_rows // P_SIZE
    width = weight.shape[-1]
    step = GROUP * WW
    return pl.pallas_call(
        embed_kernel,
        grid=(columns // step,),
        in_specs=[
            pl.BlockSpec((pixel_rows, step, chans), lambda g: (0, g, 0)),
            pl.BlockSpec(affine.shape, lambda g: (0, 0)),
            pl.BlockSpec(weight.shape, lambda g: (0,) * weight.ndim),
            pl.BlockSpec(weight.shape, lambda g: (0,) * weight.ndim),
        ],
        out_specs=[
            pl.BlockSpec((HALO, step, width), lambda g: (0, g, 0)),
            pl.BlockSpec((HALO, step, width), lambda g: (0, g, 0)),
            pl.BlockSpec((rows * step, width), lambda g: (g, 0)),
        ],
        out_shape=[
            jax.ShapeDtypeStruct((HALO, columns, width), BF16),
            jax.ShapeDtypeStruct((HALO, columns, width), BF16),
            jax.ShapeDtypeStruct((rows * columns, width), BF16),
        ],
        scratch_shapes=[
            pltpu.VMEM((P_SIZE, chans, width), BF16),
            pltpu.VMEM((rows * step, rows * step), BF16),
        ],
        compiler_params=pltpu.CompilerParams(vmem_limit_bytes=16 * 1024 * 1024),
        cost_estimate=pl.CostEstimate(
            flops=EMBED_COST,
            bytes_accessed=0,
            transcendentals=0,
        ),
        name="embed",
    )(fields, affine, weight, other)


def roll_matrix(columns, shift, scale):
    slots = columns // WW * PAD
    row = lax.broadcasted_iota(jnp.int32, (slots, 1), 0)
    column = lax.broadcasted_iota(jnp.int32, (slots, columns), 1)
    place = row % PAD
    want = (row // PAD) * WW + place + shift
    want = jnp.where(want >= columns, want - columns, want)
    want = jnp.where(place < WW, want, columns)
    return jnp.where(column == want, scale, 0.0).astype(BF16)


def project_kernel(
    column_offset_ref,
    top_ref,
    bottom_ref,
    weight_ref,
    other_ref,
    query_ref,
    key_value_ref,
    matrix_ref,
    query_matrix_ref,
):
    rows = query_ref.shape[0]
    columns, features = top_ref.shape[1:]
    width = query_ref.shape[-1]
    shift = column_offset_ref[position()["lon"]]
    refs = weight_ref, other_ref
    collect(parts(refs, 0, LINES, 2 * LINES), matrix_ref)
    for spot, block in parts(refs, LINES, LINES, 2 * LINES):
        block = block.astype(F32)[:, LINES // 2 :]
        block = jnp.concatenate([block[..., :width], block[..., width:]], axis=1)
        collect([(spot, block.reshape(-1, width).astype(BF16))], query_matrix_ref)
    matrix = jnp.concatenate([query_matrix_ref[...], matrix_ref[...]], axis=1)
    to_windows = roll_matrix(columns, shift, 1.0)
    to_queries = roll_matrix(columns, shift, HEAD_DIM**-0.5)
    for row in range(rows):
        values = top_ref[row] if row < HALO else bottom_ref[row - rows + HALO]
        normed = layer_norm(values.astype(F32))
        projected = dot(normed, matrix).astype(BF16)
        query_ref[row] = dot(to_queries, projected[:, :width]).astype(BF16)
        key_value_ref[row] = dot(to_windows, projected[:, width:]).astype(BF16)


def project(column_offset, top, bottom, weights):
    rows = WH
    columns, features = top.shape[1:]
    width = HEADS * HEAD_DIM
    slots = columns // WW * PAD
    return pl.pallas_call(
        project_kernel,
        in_specs=[pl.BlockSpec(memory_space=pltpu.SMEM)]
        + [pl.BlockSpec(memory_space=pltpu.VMEM)] * 4,
        out_shape=[
            jax.ShapeDtypeStruct((rows, slots, width), BF16),
            jax.ShapeDtypeStruct((rows, slots, 2 * width), BF16),
            jax.ShapeDtypeStruct((features, 2 * width), BF16),
        ],
        scratch_shapes=[pltpu.VMEM((features, width), BF16)],
        compiler_params=pltpu.CompilerParams(vmem_limit_bytes=20 * 1024 * 1024),
        cost_estimate=pl.CostEstimate(
            flops=2 * rows * columns * (features + slots) * 3 * width,
            bytes_accessed=rows * columns * features * 2 + rows * slots * 3 * width * 2,
            transcendentals=0,
        ),
        name="project",
    )(column_offset, top, bottom, *weights)


def attend_kernel(
    row_offset_ref,
    column_offset_ref,
    north_ref,
    south_ref,
    query_ref,
    own_ref,
    matrix_ref,
    mixed_ref,
    keys_ref,
    made_ref,
):
    rows, slots, width = query_ref.shape
    columns = north_ref.shape[1]
    windows = slots // PAD
    here = position()
    lat, last = here["lat"], here["last"]
    split, shift = row_offset_ref[here["lon"]], column_offset_ref[here["lon"]]
    half = keys_ref.shape[0] // 2
    for band in range(2):
        for slot in range(rows, half):
            keys_ref[band * half + slot] = jnp.zeros(keys_ref.shape[1:], BF16)
    for row in range(rows):
        spot = jnp.where(row < split, row + rows - split, half + row - split)
        keys_ref[spot] = own_ref[row]

    matrix = matrix_ref[...]
    to_windows = roll_matrix(columns, shift, 1.0)
    for slot in range(rows):
        above = slot < rows - split
        north = north_ref[jnp.minimum(split - 1 + slot, HALO - 1)]
        south = south_ref[jnp.maximum(slot - (rows - split), 0)]
        values = jnp.where(above, north.astype(F32), south.astype(F32))
        projected = dot(layer_norm(values), matrix).astype(BF16)
        spot = jnp.where(above, slot, half + slot)
        keys_ref[spot] = dot(to_windows, projected).astype(BF16)

    shape = (rows, PAD, half * PAD)
    north_query = lax.broadcasted_iota(jnp.int32, shape, 0) < split
    key = lax.broadcasted_iota(jnp.int32, shape, 2)
    key_row = key // PAD
    from_north = key_row < rows - split
    beyond = jnp.where(
        north_query, jnp.where(from_north, lat, 1), jnp.where(from_north, 1, last - lat)
    )
    bias = jnp.where((key_row < rows) & (key % PAD < WW) & (beyond > 0), 0.0, -1e30)
    lane_head = lax.broadcasted_iota(jnp.int32, (rows * PAD, width), 1) // HEAD_DIM

    def window(m):
        here = pl.ds(pl.multiple_of(m * PAD, PAD), PAD)
        queries = query_ref[:, here, :].reshape(rows * PAD, width)
        keys = keys_ref[:, here, :].reshape(2 * half * PAD, 2 * width)
        zero = jnp.zeros_like(queries)
        stacked = jnp.concatenate(
            [jnp.where(lane_head == head, queries, zero) for head in range(HEADS)], axis=0
        )
        scores = dot_nt(stacked, keys[:, :width]).reshape(HEADS, rows, PAD, 2 * half * PAD)
        scores = jnp.where(north_query[None], scores[..., : half * PAD], scores[..., half * PAD :])
        scores = scores + bias[None]
        weights = jnp.exp(scores - jnp.max(scores, axis=-1, keepdims=True))
        weights = weights * (1.0 / jnp.sum(weights, axis=-1, keepdims=True))
        weights = jnp.concatenate(
            [jnp.where(north_query[None], weights, 0.0), jnp.where(north_query[None], 0.0, weights)],
            axis=-1,
        ).astype(BF16)
        products = dot(weights.reshape(HEADS * rows * PAD, -1), keys[:, width:])
        products = products.reshape(HEADS, rows * PAD, width)
        mixed = products[0]
        for head in range(1, HEADS):
            mixed = jnp.where(lane_head == head, products[head], mixed)
        mixed = mixed.astype(BF16).reshape(rows, PAD, width)
        made_ref[:, pl.ds(pl.multiple_of((m + 1) * PAD, PAD), PAD), :] = mixed

    def some_windows(step, carry):
        for inner in range(GROUP):
            window(step * GROUP + inner)
        return carry

    lax.fori_loop(0, windows // GROUP, some_windows, 0)
    made_ref[:, :PAD, :] = made_ref[:, windows * PAD :, :]

    def source(k):
        row, column = k // WW, k % WW
        inner = jnp.where(column < shift, column + WW - shift, PAD + column - shift)
        return row * (2 * PAD) + inner

    back = one_hot((rows * WW, rows * 2 * PAD), source)
    for j in range(windows):
        pair = made_ref[:, j * PAD : (j + 2) * PAD, :]
        mixed_ref[j] = dot(back, pair.reshape(rows * 2 * PAD, width)).astype(BF16)


def attend(row_offset, column_offset, north, south, queries, own, matrix):
    rows, slots, width = queries.shape
    windows = slots // PAD
    columns, features = north.shape[1:]
    vmem = pl.BlockSpec(memory_space=pltpu.VMEM)
    return pl.pallas_call(
        attend_kernel,
        in_specs=[pl.BlockSpec(memory_space=pltpu.SMEM)] * 2 + [vmem] * 5,
        out_shape=jax.ShapeDtypeStruct((windows, rows * WW, width), BF16),
        scratch_shapes=[
            pltpu.VMEM((2 * BAND, slots, 2 * width), BF16),
            pltpu.VMEM((rows, slots + PAD, width), BF16),
        ],
        compiler_params=pltpu.CompilerParams(vmem_limit_bytes=24 * 1024 * 1024),
        cost_estimate=pl.CostEstimate(
            flops=ATTEND_COST * 2 * rows * columns * (features + slots) * 2 * width
            + ATTEND_COST * 4 * windows * HEADS * rows * PAD * 2 * rows * PAD * width,
            bytes_accessed=2 * north.size * 2 + rows * slots * 4 * width * 2,
            transcendentals=windows * HEADS * rows * PAD * 2 * rows * PAD,
        ),
        name="attend",
    )(row_offset, column_offset, north, south, queries, own, matrix)


def finish_kernel(
    tokens_ref,
    mixed_ref,
    hidden_ref,
    hidden_other_ref,
    near_ref,
    near_other_ref,
    encoded_ref,
    out_ref,
    first_ref,
    second_ref,
    order_ref,
):
    count, cells, features = tokens_ref.shape
    lines = LINES

    @pl.when(pl.program_id(0) == 0)
    def _():
        refs = hidden_ref, hidden_other_ref
        collect(parts(refs, 0, lines, 4 * lines), first_ref, slice(0, features))
        collect(parts(refs, lines, lines, 4 * lines), first_ref, slice(features, 2 * features))
        collect(parts(refs, 2 * lines, 2 * lines, 4 * lines), second_ref)
        for spot, block in parts((near_ref, near_other_ref), lines, lines, 2 * lines):
            block = block.astype(F32)[:, : lines // 2].reshape(-1, features)
            collect([(spot, block.astype(BF16))], out_ref)
        order_ref[...] = one_hot(order_ref.shape, lambda k: (k % count) * cells + k // count)

    tokens = tokens_ref[...].astype(F32).reshape(count * cells, features)
    mixed = mixed_ref[...].astype(F32).reshape(count * cells, -1).astype(BF16)
    residual = tokens + dot(mixed, out_ref[...])
    inner = layer_norm(residual)
    expanded = jax.nn.gelu(dot(inner, first_ref[...]), approximate=True).astype(BF16)
    encoded = (residual + dot(expanded, second_ref[...])).astype(BF16)
    encoded_ref[...] = dot(order_ref[...], encoded).astype(BF16).reshape(cells, count, features)


def finish(tokens, mixed, weights):
    count, cells, features = tokens.shape
    width = mixed.shape[2]
    hidden = 2 * features
    block = 24
    return pl.pallas_call(
        finish_kernel,
        grid=(cells // block,),
        in_specs=[
            pl.BlockSpec((count, block, features), lambda g: (0, g, 0)),
            pl.BlockSpec((count, block, width), lambda g: (0, g, 0)),
        ]
        + [pl.BlockSpec(weight.shape, lambda g: (0, 0, 0)) for weight in weights],
        out_specs=pl.BlockSpec((block, count, features), lambda g: (g, 0, 0)),
        out_shape=jax.ShapeDtypeStruct((cells, count, features), BF16),
        scratch_shapes=[
            pltpu.VMEM((width, features), BF16),
            pltpu.VMEM((features, hidden), BF16),
            pltpu.VMEM((hidden, features), BF16),
            pltpu.VMEM((count * block, count * block), BF16),
        ],
        compiler_params=pltpu.CompilerParams(vmem_limit_bytes=24 * 1024 * 1024),
        cost_estimate=pl.CostEstimate(
            flops=2 * count * cells * features * (width + 2 * hidden),
            bytes_accessed=count * cells * (4 * features + 2 * width) + weights[0].size * 6,
            transcendentals=count * cells * hidden,
        ),
        name="finish",
    )(tokens, mixed, *weights)


def swap(values, axis):
    return lax.ppermute(values, axis, [(0, 1), (1, 0)])


def after(first, *later):
    return lax.optimization_barrier((first,) + later)


def shards(
    fields,
    scale_exponent,
    level_mean,
    level_spread,
    row_offset,
    column_offset,
    patch_weight,
    attention_in,
    attention_out,
    hidden_in,
    hidden_out,
):
    features = patch_weight.shape[1]
    chans = fields.shape[3]
    lats = lax.axis_size("lat")
    repeat = chans // level_mean.shape[0]
    affine = jnp.stack(
        [
            jnp.tile(jnp.exp2(scale_exponent.astype(F32)) / level_spread, repeat),
            jnp.tile(level_mean / level_spread, repeat),
        ]
    )

    far = lax.axis_size("y_lo"), lats
    patch, packed = pack(
        far[0] * far[1], patch_weight, hidden_in, hidden_out, attention_out, attention_in
    )
    packed = join(packed, swap(packed, "y_lo"))
    rest = lax.all_gather(packed, "lat", axis=0)
    patch = lax.all_to_all(patch, ("y_lo", "lat"), 0, 0, tiled=True)
    patch = patch.reshape(far + patch_weight.shape)

    top, bottom, tiles = embed(fields[0], affine, patch, swap(patch, "core"))
    _, rest = after(top, rest)
    north = lax.ppermute(bottom, "lat", [(i, i + 1) for i in range(lats - 1)])
    south = lax.ppermute(top, "lat", [(i + 1, i) for i in range(lats - 1)])
    tiles = tiles.reshape(-1, WH * WW, features)
    tile_tokens = lax.all_to_all(tiles, ("y_hi", "x"), 0, 0, tiled=True)

    near = rest[:, 8 * LINES :]
    near = near, swap(near, "core")
    window_queries, own, matrix = project(column_offset, top, bottom, near)
    mixed = attend(row_offset, column_offset, north, south, window_queries, own, matrix)
    _, mixed = after(tile_tokens, mixed)
    _, hidden_weight = after(mixed, rest[:, : 8 * LINES])
    tile_mixed = lax.all_to_all(mixed, ("y_hi", "x"), 0, 0, tiled=True)
    encoded = finish(tile_tokens, tile_mixed, (hidden_weight, swap(hidden_weight, "core")) + near)
    return encoded.reshape(WH, WW, -1, features).transpose(2, 0, 1, 3)


def solution(mesh):
    tm, lat, lon = (mesh.shape[name] for name in ("tm", "lat", "lon"))
    cores, across = 2, 4
    finer = Mesh(
        mesh.devices.reshape(tm // cores, cores, lat, lon // across, across),
        ("y_lo", "core", "lat", "y_hi", "x"),
    )
    time = ("y_lo", "core")
    in_specs = (
        P(time + ("y_hi", "x"), "lat", None, None),
        P(),
        P(),
        P(),
        P(time),
        P(time),
        P(time + ("lat",), None),
        P(time + ("lat",), None),
        P(time + ("lat",), None),
        P(time + ("lat",), None),
        P(time + ("lat",), None),
    )
    out_specs = P(time, "lat", ("y_hi", "x"), None)
    return jax.shard_map(shards, mesh=finer, in_specs=in_specs, out_specs=out_specs, check_vma=False)
```

```python
import functools

import jax
import jax.numpy as jnp
from jax import lax
from jax.experimental import pallas as pl
from jax.experimental.pallas import tpu as pltpu
from jax.sharding import Mesh
from jax.sharding import PartitionSpec as P

P_SIZE = 4
HEAD_DIM = 64
HEADS = 4
WH = 6
WW = 12
PAD = 16
HALO = WH - 1
BAND = 8
EPSILON = 1e-05
BF16 = jnp.bfloat16
F32 = jnp.float32
GROUP = 4
ATTEND_COST = 5
EMBED_COST = 8 * 10**9
UNROLL = 16
LINES = 16


def dot(a, b):
    return jnp.dot(a, b, preferred_element_type=F32)


def dot_nt(a, b):
    return lax.dot_general(a, b, (((1,), (1,)), ((), ())), preferred_element_type=F32)


def one_hot(shape, column_of_row):
    row = lax.broadcasted_iota(jnp.int32, (shape[0], 1), 0)
    column = lax.broadcasted_iota(jnp.int32, shape, 1)
    return jnp.where(column == column_of_row(row), 1.0, 0.0).astype(BF16)


def layer_norm(values):
    center = values - jnp.mean(values, axis=-1, keepdims=True)
    spread = jnp.mean(center * center, axis=-1, keepdims=True)
    return (center * lax.rsqrt(spread + EPSILON)).astype(BF16)


def position():
    lon = lax.axis_index("y_hi") * lax.axis_size("x") + lax.axis_index("x")
    return {
        "core": lax.axis_index("core"),
        "y_lo": lax.axis_index("y_lo"),
        "lat": lax.axis_index("lat"),
        "last": lax.axis_size("lat") - 1,
        "lon": lon,
    }


def place(core_swapped, y_swapped):
    here = position()
    core, y = here["core"], here["y_lo"]
    core = 1 - core if core_swapped else core
    y = 1 - y if y_swapped else y
    return y * 2 + core


def collect(shards, target_ref, columns=slice(None)):
    for spot, block in shards:
        block = block.reshape(-1, block.shape[-1])
        start = pl.multiple_of(spot * block.shape[0], block.shape[0])
        target_ref[pl.ds(start, block.shape[0]), columns] = block


def parts(refs, first, count, half):
    return [
        (place(swapped, y), ref[:, y * half + first : y * half + first + count])
        for swapped, ref in enumerate(refs)
        for y in range(2)
    ]


def pack_kernel(
    patch_ref, hidden_in_ref, hidden_out_ref, attention_out_ref, attention_in_ref, copies_ref, packed_ref
):
    for k in range(copies_ref.shape[0]):
        copies_ref[k] = patch_ref[...]
    lines, features = LINES, packed_ref.shape[1]
    short = lines // 2
    width = attention_in_ref.shape[1] // 3
    packed_ref[:lines] = hidden_in_ref[:, :features]
    packed_ref[lines : 2 * lines] = hidden_in_ref[:, features:]
    packed_ref[2 * lines : 4 * lines] = hidden_out_ref[...]
    packed_ref[4 * lines : 5 * lines] = attention_in_ref[:, width:]
    query = attention_in_ref[:, :width].astype(F32)
    query = jnp.concatenate([query[:short], query[short:]], axis=1)
    out = attention_out_ref[...].astype(F32)
    packed_ref[5 * lines :] = jnp.concatenate([out, query], axis=0).astype(BF16)


def pack(count, patch, hidden_in, hidden_out, attention_out, attention_in):
    return pl.pallas_call(
        pack_kernel,
        in_specs=[pl.BlockSpec(memory_space=pltpu.VMEM)] * 5,
        out_shape=[
            jax.ShapeDtypeStruct((count,) + patch.shape, BF16),
            jax.ShapeDtypeStruct((6 * LINES, hidden_out.shape[1]), BF16),
        ],
        name="pack",
    )(patch, hidden_in, hidden_out, attention_out, attention_in)


def join_kernel(own_ref, swapped_ref, joined_ref):
    far = 4 * LINES
    near = own_ref.shape[0] - far
    joined_ref[:far] = own_ref[:far]
    joined_ref[far : 2 * far] = swapped_ref[:far]
    joined_ref[2 * far : 2 * far + near] = own_ref[far:]
    joined_ref[2 * far + near :] = swapped_ref[far:]


def join(own, swapped):
    return pl.pallas_call(
        join_kernel,
        in_specs=[pl.BlockSpec(memory_space=pltpu.VMEM)] * 2,
        out_shape=jax.ShapeDtypeStruct((2 * own.shape[0], own.shape[1]), BF16),
        name="join",
    )(own, swapped)


def embed_kernel(
    fields_ref,
    affine_ref,
    weight_ref,
    other_ref,
    top_ref,
    bottom_ref,
    tiles_ref,
    table_ref,
    order_ref,
):
    rows = fields_ref.shape[0] // P_SIZE
    columns = fields_ref.shape[1]

    def source(k):
        tile, inner = k // (rows * WW), k % (rows * WW)
        return (inner // WW) * columns + tile * WW + inner % WW

    @pl.when(pl.program_id(0) == 0)
    def _():
        for swapped, ref in enumerate((weight_ref, other_ref)):
            for y in range(ref.shape[0]):
                core = place(swapped, 0) % 2
                table_ref[2 * y + core] = ref[y].reshape(table_ref.shape[1:])
        order_ref[...] = one_hot(order_ref.shape, source)

    chans = fields_ref.shape[2]
    raw = fields_ref[...].reshape(rows, P_SIZE, columns, chans)
    factor = affine_ref[0:1, :]
    shift = affine_ref[1:2, :]
    total = None
    for pixel in range(P_SIZE):
        part = raw[:, pixel].reshape(rows * columns, chans).astype(F32)
        part = (part * factor - shift).astype(BF16)
        product = dot(part, table_ref[pixel])
        total = product if total is None else total + product
    tokens = total.astype(BF16)
    by_row = tokens.reshape(rows, columns, -1)
    top_ref[...] = by_row[:HALO]
    bottom_ref[...] = by_row[rows - HALO :]

    tiles_ref[...] = dot(order_ref[...], tokens).astype(BF16)


def embed(fields, affine, weight, other):
    pixel_rows, columns, chans = fields.shape
    rows = pixel_rows // P_SIZE
    width = weight.shape[-1]
    step = GROUP * WW
    return pl.pallas_call(
        embed_kernel,
        grid=(columns // step,),
        in_specs=[
            pl.BlockSpec((pixel_rows, step, chans), lambda g: (0, g, 0)),
            pl.BlockSpec(affine.shape, lambda g: (0, 0)),
            pl.BlockSpec(weight.shape, lambda g: (0,) * weight.ndim),
            pl.BlockSpec(weight.shape, lambda g: (0,) * weight.ndim),
        ],
        out_specs=[
            pl.BlockSpec((HALO, step, width), lambda g: (0, g, 0)),
            pl.BlockSpec((HALO, step, width), lambda g: (0, g, 0)),
            pl.BlockSpec((rows * step, width), lambda g: (g, 0)),
        ],
        out_shape=[
            jax.ShapeDtypeStruct((HALO, columns, width), BF16),
            jax.ShapeDtypeStruct((HALO, columns, width), BF16),
            jax.ShapeDtypeStruct((rows * columns, width), BF16),
        ],
        scratch_shapes=[
            pltpu.VMEM((P_SIZE, chans, width), BF16),
            pltpu.VMEM((rows * step, rows * step), BF16),
        ],
        compiler_params=pltpu.CompilerParams(vmem_limit_bytes=16 * 1024 * 1024),
        cost_estimate=pl.CostEstimate(
            flops=EMBED_COST,
            bytes_accessed=0,
            transcendentals=0,
        ),
        name="embed",
    )(fields, affine, weight, other)


def roll_matrix(columns, shift, scale):
    slots = columns // WW * PAD
    row = lax.broadcasted_iota(jnp.int32, (slots, 1), 0)
    column = lax.broadcasted_iota(jnp.int32, (slots, columns), 1)
    place = row % PAD
    want = (row // PAD) * WW + place + shift
    want = jnp.where(want >= columns, want - columns, want)
    want = jnp.where(place < WW, want, columns)
    return jnp.where(column == want, scale, 0.0).astype(BF16)


def project_kernel(
    column_offset_ref,
    top_ref,
    bottom_ref,
    weight_ref,
    other_ref,
    query_ref,
    key_value_ref,
    matrix_ref,
    query_matrix_ref,
):
    rows = query_ref.shape[0]
    columns, features = top_ref.shape[1:]
    width = query_ref.shape[-1]
    shift = column_offset_ref[position()["lon"]]
    refs = weight_ref, other_ref
    collect(parts(refs, 0, LINES, 2 * LINES), matrix_ref)
    for spot, block in parts(refs, LINES, LINES, 2 * LINES):
        block = block.astype(F32)[:, LINES // 2 :]
        block = jnp.concatenate([block[..., :width], block[..., width:]], axis=1)
        collect([(spot, block.reshape(-1, width).astype(BF16))], query_matrix_ref)
    matrix = jnp.concatenate([query_matrix_ref[...], matrix_ref[...]], axis=1)
    to_windows = roll_matrix(columns, shift, 1.0)
    to_queries = roll_matrix(columns, shift, HEAD_DIM**-0.5)
    for row in range(rows):
        values = top_ref[row] if row < HALO else bottom_ref[row - rows + HALO]
        normed = layer_norm(values.astype(F32))
        projected = dot(normed, matrix).astype(BF16)
        query_ref[row] = dot(to_queries, projected[:, :width]).astype(BF16)
        key_value_ref[row] = dot(to_windows, projected[:, width:]).astype(BF16)


def project(column_offset, top, bottom, weights):
    rows = WH
    columns, features = top.shape[1:]
    width = HEADS * HEAD_DIM
    slots = columns // WW * PAD
    return pl.pallas_call(
        project_kernel,
        in_specs=[pl.BlockSpec(memory_space=pltpu.SMEM)]
        + [pl.BlockSpec(memory_space=pltpu.VMEM)] * 4,
        out_shape=[
            jax.ShapeDtypeStruct((rows, slots, width), BF16),
            jax.ShapeDtypeStruct((rows, slots, 2 * width), BF16),
            jax.ShapeDtypeStruct((features, 2 * width), BF16),
        ],
        scratch_shapes=[pltpu.VMEM((features, width), BF16)],
        compiler_params=pltpu.CompilerParams(vmem_limit_bytes=20 * 1024 * 1024),
        cost_estimate=pl.CostEstimate(
            flops=2 * rows * columns * (features + slots) * 3 * width,
            bytes_accessed=rows * columns * features * 2 + rows * slots * 3 * width * 2,
            transcendentals=0,
        ),
        name="project",
    )(column_offset, top, bottom, *weights)


def attend_kernel(
    row_offset_ref,
    column_offset_ref,
    north_ref,
    south_ref,
    query_ref,
    own_ref,
    matrix_ref,
    mixed_ref,
    keys_ref,
    made_ref,
):
    rows, slots, width = query_ref.shape
    columns = north_ref.shape[1]
    windows = slots // PAD
    here = position()
    lat, last = here["lat"], here["last"]
    split, shift = row_offset_ref[here["lon"]], column_offset_ref[here["lon"]]
    half = keys_ref.shape[0] // 2
    for band in range(2):
        for slot in range(rows, half):
            keys_ref[band * half + slot] = jnp.zeros(keys_ref.shape[1:], BF16)
    for row in range(rows):
        spot = jnp.where(row < split, row + rows - split, half + row - split)
        keys_ref[spot] = own_ref[row]

    matrix = matrix_ref[...]
    to_windows = roll_matrix(columns, shift, 1.0)
    for slot in range(rows):
        above = slot < rows - split
        north = north_ref[jnp.minimum(split - 1 + slot, HALO - 1)]
        south = south_ref[jnp.maximum(slot - (rows - split), 0)]
        values = jnp.where(above, north.astype(F32), south.astype(F32))
        projected = dot(layer_norm(values), matrix).astype(BF16)
        spot = jnp.where(above, slot, half + slot)
        keys_ref[spot] = dot(to_windows, projected).astype(BF16)

    shape = (rows, PAD, half * PAD)
    north_query = lax.broadcasted_iota(jnp.int32, shape, 0) < split
    key = lax.broadcasted_iota(jnp.int32, shape, 2)
    key_row = key // PAD
    from_north = key_row < rows - split
    beyond = jnp.where(
        north_query, jnp.where(from_north, lat, 1), jnp.where(from_north, 1, last - lat)
    )
    bias = jnp.where((key_row < rows) & (key % PAD < WW) & (beyond > 0), 0.0, -1e30)
    lane_head = lax.broadcasted_iota(jnp.int32, (rows * PAD, width), 1) // HEAD_DIM

    def window(m):
        here = pl.ds(pl.multiple_of(m * PAD, PAD), PAD)
        queries = query_ref[:, here, :].reshape(rows * PAD, width)
        keys = keys_ref[:, here, :].reshape(2 * half * PAD, 2 * width)
        zero = jnp.zeros_like(queries)
        stacked = jnp.concatenate(
            [jnp.where(lane_head == head, queries, zero) for head in range(HEADS)], axis=0
        )
        scores = dot_nt(stacked, keys[:, :width]).reshape(HEADS, rows, PAD, 2 * half * PAD)
        scores = jnp.where(north_query[None], scores[..., : half * PAD], scores[..., half * PAD :])
        scores = scores + bias[None]
        weights = jnp.exp(scores - jnp.max(scores, axis=-1, keepdims=True))
        weights = weights * (1.0 / jnp.sum(weights, axis=-1, keepdims=True))
        weights = jnp.concatenate(
            [jnp.where(north_query[None], weights, 0.0), jnp.where(north_query[None], 0.0, weights)],
            axis=-1,
        ).astype(BF16)
        products = dot(weights.reshape(HEADS * rows * PAD, -1), keys[:, width:])
        products = products.reshape(HEADS, rows * PAD, width)
        mixed = products[0]
        for head in range(1, HEADS):
            mixed = jnp.where(lane_head == head, products[head], mixed)
        mixed = mixed.astype(BF16).reshape(rows, PAD, width)
        made_ref[:, pl.ds(pl.multiple_of((m + 1) * PAD, PAD), PAD), :] = mixed

    def some_windows(step, carry):
        for inner in range(UNROLL):
            window(step * UNROLL + inner)
        return carry

    lax.fori_loop(0, windows // UNROLL, some_windows, 0)
    made_ref[:, :PAD, :] = made_ref[:, windows * PAD :, :]

    def source(k):
        row, column = k // WW, k % WW
        inner = jnp.where(column < shift, column + WW - shift, PAD + column - shift)
        return row * (2 * PAD) + inner

    back = one_hot((rows * WW, rows * 2 * PAD), source)
    for j in range(windows):
        pair = made_ref[:, j * PAD : (j + 2) * PAD, :]
        mixed_ref[j] = dot(back, pair.reshape(rows * 2 * PAD, width)).astype(BF16)


def attend(row_offset, column_offset, north, south, queries, own, matrix):
    rows, slots, width = queries.shape
    windows = slots // PAD
    columns, features = north.shape[1:]
    vmem = pl.BlockSpec(memory_space=pltpu.VMEM)
    return pl.pallas_call(
        attend_kernel,
        in_specs=[pl.BlockSpec(memory_space=pltpu.SMEM)] * 2 + [vmem] * 5,
        out_shape=jax.ShapeDtypeStruct((windows, rows * WW, width), BF16),
        scratch_shapes=[
            pltpu.VMEM((2 * BAND, slots, 2 * width), BF16),
            pltpu.VMEM((rows, slots + PAD, width), BF16),
        ],
        compiler_params=pltpu.CompilerParams(vmem_limit_bytes=24 * 1024 * 1024),
        cost_estimate=pl.CostEstimate(
            flops=ATTEND_COST * 2 * rows * columns * (features + slots) * 2 * width
            + ATTEND_COST * 4 * windows * HEADS * rows * PAD * 2 * rows * PAD * width,
            bytes_accessed=2 * north.size * 2 + rows * slots * 4 * width * 2,
            transcendentals=windows * HEADS * rows * PAD * 2 * rows * PAD,
        ),
        name="attend",
    )(row_offset, column_offset, north, south, queries, own, matrix)


def finish_kernel(
    tokens_ref,
    mixed_ref,
    hidden_ref,
    hidden_other_ref,
    near_ref,
    near_other_ref,
    encoded_ref,
    out_ref,
    first_ref,
    second_ref,
    order_ref,
):
    count, cells, features = tokens_ref.shape
    lines = LINES

    @pl.when(pl.program_id(0) == 0)
    def _():
        refs = hidden_ref, hidden_other_ref
        collect(parts(refs, 0, lines, 4 * lines), first_ref, slice(0, features))
        collect(parts(refs, lines, lines, 4 * lines), first_ref, slice(features, 2 * features))
        collect(parts(refs, 2 * lines, 2 * lines, 4 * lines), second_ref)
        for spot, block in parts((near_ref, near_other_ref), lines, lines, 2 * lines):
            block = block.astype(F32)[:, : lines // 2].reshape(-1, features)
            collect([(spot, block.astype(BF16))], out_ref)
        order_ref[...] = one_hot(order_ref.shape, lambda k: (k % count) * cells + k // count)

    tokens = tokens_ref[...].astype(F32).reshape(count * cells, features)
    mixed = mixed_ref[...].astype(F32).reshape(count * cells, -1).astype(BF16)
    residual = tokens + dot(mixed, out_ref[...])
    inner = layer_norm(residual)
    expanded = jax.nn.gelu(dot(inner, first_ref[...]), approximate=True).astype(BF16)
    encoded = (residual + dot(expanded, second_ref[...])).astype(BF16)
    encoded_ref[...] = dot(order_ref[...], encoded).astype(BF16).reshape(cells, count, features)


def finish(tokens, mixed, weights):
    count, cells, features = tokens.shape
    width = mixed.shape[2]
    hidden = 2 * features
    block = 72
    return pl.pallas_call(
        finish_kernel,
        grid=(cells // block,),
        in_specs=[
            pl.BlockSpec((count, block, features), lambda g: (0, g, 0)),
            pl.BlockSpec((count, block, width), lambda g: (0, g, 0)),
        ]
        + [pl.BlockSpec(weight.shape, lambda g: (0, 0, 0)) for weight in weights],
        out_specs=pl.BlockSpec((block, count, features), lambda g: (g, 0, 0)),
        out_shape=jax.ShapeDtypeStruct((cells, count, features), BF16),
        scratch_shapes=[
            pltpu.VMEM((width, features), BF16),
            pltpu.VMEM((features, hidden), BF16),
            pltpu.VMEM((hidden, features), BF16),
            pltpu.VMEM((count * block, count * block), BF16),
        ],
        compiler_params=pltpu.CompilerParams(vmem_limit_bytes=40 * 1024 * 1024),
        cost_estimate=pl.CostEstimate(
            flops=2 * count * cells * features * (width + 2 * hidden),
            bytes_accessed=count * cells * (4 * features + 2 * width) + weights[0].size * 6,
            transcendentals=count * cells * hidden,
        ),
        name="finish",
    )(tokens, mixed, *weights)


def swap(values, axis):
    return lax.ppermute(values, axis, [(0, 1), (1, 0)])


def after(first, *later):
    return lax.optimization_barrier((first,) + later)


def shards(
    fields,
    scale_exponent,
    level_mean,
    level_spread,
    row_offset,
    column_offset,
    patch_weight,
    attention_in,
    attention_out,
    hidden_in,
    hidden_out,
):
    features = patch_weight.shape[1]
    chans = fields.shape[3]
    lats = lax.axis_size("lat")
    repeat = chans // level_mean.shape[0]
    affine = jnp.stack(
        [
            jnp.tile(jnp.exp2(scale_exponent.astype(F32)) / level_spread, repeat),
            jnp.tile(level_mean / level_spread, repeat),
        ]
    )

    far = lax.axis_size("y_lo"), lats
    patch, packed = pack(
        far[0] * far[1], patch_weight, hidden_in, hidden_out, attention_out, attention_in
    )
    packed = join(packed, swap(packed, "y_lo"))
    rest = lax.all_gather(packed, "lat", axis=0)
    patch = lax.all_to_all(patch, ("y_lo", "lat"), 0, 0, tiled=True)
    patch = patch.reshape(far + patch_weight.shape)

    top, bottom, tiles = embed(fields[0], affine, patch, swap(patch, "core"))
    _, rest = after(top, rest)
    north = lax.ppermute(bottom, "lat", [(i, i + 1) for i in range(lats - 1)])
    south = lax.ppermute(top, "lat", [(i + 1, i) for i in range(lats - 1)])
    tiles = tiles.reshape(-1, WH * WW, features)
    tile_tokens = lax.all_to_all(tiles, ("y_hi", "x"), 0, 0, tiled=True)

    near = rest[:, 8 * LINES :]
    near = near, swap(near, "core")
    window_queries, own, matrix = project(column_offset, top, bottom, near)
    mixed = attend(row_offset, column_offset, north, south, window_queries, own, matrix)
    _, mixed = after(tile_tokens, mixed)
    _, hidden_weight = after(mixed, rest[:, : 8 * LINES])
    tile_mixed = lax.all_to_all(mixed, ("y_hi", "x"), 0, 0, tiled=True)
    encoded = finish(tile_tokens, tile_mixed, (hidden_weight, swap(hidden_weight, "core")) + near)
    return encoded.reshape(WH, WW, -1, features).transpose(2, 0, 1, 3)


def solution(mesh):
    tm, lat, lon = (mesh.shape[name] for name in ("tm", "lat", "lon"))
    cores, across = 2, 4
    finer = Mesh(
        mesh.devices.reshape(tm // cores, cores, lat, lon // across, across),
        ("y_lo", "core", "lat", "y_hi", "x"),
    )
    time = ("y_lo", "core")
    in_specs = (
        P(time + ("y_hi", "x"), "lat", None, None),
        P(),
        P(),
        P(),
        P(time),
        P(time),
        P(time + ("lat",), None),
        P(time + ("lat",), None),
        P(time + ("lat",), None),
        P(time + ("lat",), None),
        P(time + ("lat",), None),
    )
    out_specs = P(time, "lat", ("y_hi", "x"), None)
    return jax.shard_map(shards, mesh=finer, in_specs=in_specs, out_specs=out_specs, check_vma=False)
```
